32 devices in a mesh: tm: 4 (over y, x), feed: 8 (over z, core).
Axes of the slice: x: 2, y: 2, z: 4, core: 2. Of those that a mesh axis runs over, the one named last changes fastest.
Arguments:
- voltages: int32 [2048, 32768], P('feed', 'tm'), may hold values from -128 to 127
- feed_at_grid_slot: int32 [2048], replicated, may hold values from 0 to 2047, each once
- ew_grid: int32 [4], replicated, may hold values from 0 to 511
- ns_grid: int32 [256], replicated, may hold values from 0 to 511
- delays: int32 [1024, 512], replicated, may hold values from 0 to 15, as said below
Outputs:
- dedispersed: float32 [512, 1024, 16], P('tm', 'feed')
The draws below stay inside these ranges and needn't reach their ends.
Inputs may be any that keep to these rules, and one draw needn't show every extreme that they name: `feed_at_grid_slot`: each feed stands at exactly one grid position. delays are taken modulo 16.
All inputs are finite; a program needn't handle non-finite values.
Results may differ from the reference program's by a relative error of at most 0.017.
Values may be sent and summed in bfloat16 or wider, within the bound.
A program may use at most 128 MiB of HBM per device.

```python
import math
from functools import partial
import jax
import jax.numpy as jnp
from jax import lax

NFFT = 2048
CHANS = 1024
TAPS = 4
ROWS = 256
FEEDS = 2048
NS_BEAMS = 256
EW_BEAMS = 4
BEAMS = 1024
DMS = 512
SPECTRA = 16


def draw_delays(key, part):
    dm_key = jax.random.fold_in(key, 11)
    lag_key = jax.random.fold_in(key, 12)
    trials = jnp.arange(DMS, dtype=jnp.int32) * 4 + jax.random.randint(dm_key, (DMS,), 0, 4, dtype=jnp.int32)
    chan_ids = jnp.arange(CHANS, dtype=jnp.int32) + CHANS
    sweep_rate = 1073741824 // (chan_ids * chan_ids)
    offsets = jax.random.randint(lag_key, (CHANS,), 0, SPECTRA, dtype=jnp.int32)
    sweep_lag = jnp.right_shift(trials[None, :] * sweep_rate[:, None], 12)
    return (sweep_lag + offsets[:, None]) % SPECTRA


def touch_ends(entries, rng, least, largest):
    spot = [jax.random.randint(jax.random.fold_in(rng, axis), (), 0, length) for axis, length in enumerate(entries.shape)]
    widest = entries.shape.index(max(entries.shape))
    neighbour = spot[:widest] + [(spot[widest] + 1) % entries.shape[widest]] + spot[widest + 1:]
    return entries.at[tuple(spot)].set(least).at[tuple(neighbour)].set(largest)


def setup_inputs(seed: int = 0) -> dict:
    keys = jax.random.split(jax.random.key(seed), 6)
    return {
        "voltages": touch_ends(jax.random.randint(keys[0], (FEEDS, SPECTRA * NFFT), -128, 128), jax.random.fold_in(keys[0], 1), -128, 127).astype(jnp.int32),
        "feed_at_grid_slot": jax.random.permutation(keys[1], FEEDS).astype(jnp.int32),
        "ew_grid": touch_ends(jax.random.randint(keys[2], (EW_BEAMS,), 0, 512), jax.random.fold_in(keys[2], 1), 0, 511).astype(jnp.int32),
        "ns_grid": touch_ends(jax.random.randint(keys[3], (NS_BEAMS,), 0, 512), jax.random.fold_in(keys[3], 1), 0, 511).astype(jnp.int32),
        "delays": draw_delays(jax.random.fold_in(keys[5], 71), 0),
    }


TWO_PI = 2.0 * math.pi
phase_modulus = 1048576

def rounded_value(values):
    return lax.optimization_barrier(values.astype(jnp.bfloat16)).astype(jnp.float32)

def pfb_window(tap_count, series_length):
    points = jnp.arange(tap_count * series_length, dtype=jnp.float32) + 0.5
    start_offset = points / series_length - tap_count / 2.0
    taper = 0.5 - 0.5 * jnp.cos(TWO_PI * points / (tap_count * series_length))
    values = (jnp.sinc(start_offset) * taper).reshape(tap_count, series_length)
    return values / jnp.sqrt(lax.optimization_barrier(jnp.sum(values * values, axis=0, keepdims=True)))

def dft_table(series_length, columns):
    product = jnp.arange(series_length, dtype=jnp.int32)[:, None] * jnp.arange(columns, dtype=jnp.int32)[None, :] % series_length
    angles = product.astype(jnp.float32) * (TWO_PI / series_length)
    factor = 1.0 / math.sqrt(series_length)
    return jnp.concatenate([jnp.cos(angles) * factor, -jnp.sin(angles) * factor], axis=1).astype(jnp.bfloat16)

def spectral_table(series_length):
    product = jnp.arange(series_length, dtype=jnp.int32)[:, None] * jnp.arange(series_length, dtype=jnp.int32)[None, :] % series_length
    angles = product.astype(jnp.float32) * (TWO_PI / series_length)
    factor = 1.0 / math.sqrt(series_length)
    nonzero = (jnp.arange(series_length) > 0)[:, None]
    cosine = jnp.where(nonzero, jnp.cos(angles) * factor, 0.0)
    sine_part = jnp.where(nonzero, -jnp.sin(angles) * factor, 0.0)
    return jnp.stack([cosine, sine_part]).astype(jnp.bfloat16)

def steer_table(coords, grid_ids, chan_ids, factor):
    phases = coords[None, None, :] * grid_ids[None, :, None] * chan_ids[:, None, None] % phase_modulus
    angles = phases.astype(jnp.float32) * (TWO_PI / phase_modulus)
    return ((jnp.cos(angles) * factor).astype(jnp.bfloat16), (jnp.sin(angles) * factor).astype(jnp.bfloat16))

def form_beams(block_in, feed_at_grid_slot, ew_tables, ns_tables):
    ew_real = ew_tables[0].astype(jnp.float32)
    ew_imag = ew_tables[1].astype(jnp.float32)
    ns_real = ns_tables[0].astype(jnp.float32)
    ns_imag = ns_tables[1].astype(jnp.float32)
    item_count = block_in.shape[1]
    chan_count = block_in.shape[3]
    gridded = jnp.take(block_in, feed_at_grid_slot, axis=0).reshape(ROWS, 4, 2, item_count, 2, chan_count)
    grid_real = gridded[:, :, :, :, 0, :].astype(jnp.float32)
    grid_imag = gridded[:, :, :, :, 1, :].astype(jnp.float32)
    east_mix = partial(jnp.einsum, 'cey,rypsc->erpsc')
    east_real = rounded_value(east_mix(ew_real, grid_real) - east_mix(ew_imag, grid_imag))
    east_imag = rounded_value(east_mix(ew_real, grid_imag) + east_mix(ew_imag, grid_real))
    north_mix = partial(jnp.einsum, 'cbr,erpsc->ebpsc')
    beam_real = north_mix(ns_real, east_real) - north_mix(ns_imag, east_imag)
    beam_imag = north_mix(ns_real, east_imag) + north_mix(ns_imag, east_real)
    beam_power = lax.optimization_barrier(jnp.sum(beam_real * beam_real + beam_imag * beam_imag, axis=2))
    return beam_power.reshape(-1, item_count, chan_count).astype(jnp.bfloat16)

def reference(voltages, feed_at_grid_slot, ew_grid, ns_grid, delays):
    spec_total = voltages.shape[1] // NFFT
    window = pfb_window(TAPS, NFFT)
    twiddle = dft_table(NFFT, CHANS)
    feeds_per_block = math.gcd(FEEDS, 64)

    def channelize(block_in):
        frames = (block_in.astype(jnp.float32) / 64.0).astype(jnp.bfloat16).reshape(feeds_per_block, spec_total, NFFT)
        padded = jnp.concatenate([jnp.zeros((feeds_per_block, TAPS - 1, NFFT), jnp.bfloat16), frames], axis=1)
        filtered = jnp.zeros((feeds_per_block, spec_total, NFFT), jnp.float32)
        for tap_index in range(TAPS):
            filtered = filtered + window[tap_index] * padded[:, tap_index:tap_index + spec_total, :].astype(jnp.float32)
        result = jnp.dot(filtered.astype(jnp.bfloat16).reshape(-1, NFFT), twiddle, preferred_element_type=jnp.float32)
        return result.astype(jnp.bfloat16).reshape(feeds_per_block, spec_total, 2, CHANS)
    spectra = lax.map(channelize, voltages.reshape(FEEDS // feeds_per_block, feeds_per_block, -1))
    spectra = spectra.reshape(FEEDS, spec_total, 2, CHANS)
    chan_block = math.gcd(CHANS, 32)
    block_count = CHANS // chan_block
    gridded_everything = spectra.reshape(FEEDS, spec_total, 2, block_count, chan_block).transpose(3, 0, 1, 2, 4)

    def beam_block(inputs):
        chan_part, chan_start = inputs
        chan_ids = chan_start + jnp.arange(chan_block, dtype=jnp.int32) + CHANS
        ew_tables = steer_table(jnp.arange(4, dtype=jnp.int32), ew_grid, chan_ids, 0.5)
        ns_tables = steer_table(jnp.arange(ROWS, dtype=jnp.int32), ns_grid, chan_ids, 1.0 / math.sqrt(ROWS))
        return form_beams(chan_part, feed_at_grid_slot, ew_tables, ns_tables)
    starts = jnp.arange(block_count, dtype=jnp.int32) * chan_block
    powers = lax.map(beam_block, (gridded_everything, starts))
    intensity = powers.transpose(1, 2, 0, 3).reshape(BEAMS, spec_total, CHANS)
    time_wide = spectral_table(spec_total).astype(jnp.float32)
    freq_ids = jnp.arange(spec_total, dtype=jnp.int32)
    phases = freq_ids[:, None, None] * delays[None, :, :] % spec_total
    angles = phases.astype(jnp.float32) * (TWO_PI / spec_total)
    phase_real = rounded_value(jnp.cos(angles))
    phase_imag = rounded_value(jnp.sin(angles))
    shift_mixture = partial(jnp.einsum, 'vuw,uwt->vut')
    beam_block_size = math.gcd(BEAMS, 32)

    def search(block_in):
        freq_part = rounded_value(jnp.einsum('rkt,btc->brkc', time_wide, block_in.astype(jnp.float32)))
        spec_real = freq_part[:, 0]
        spec_imag = freq_part[:, 1]
        moved_real = shift_mixture(spec_real, phase_real) - shift_mixture(spec_imag, phase_imag)
        moved_imag = shift_mixture(spec_real, phase_imag) + shift_mixture(spec_imag, phase_real)
        folded = rounded_value(jnp.stack([moved_real, moved_imag], axis=1) * (1.0 / math.sqrt(CHANS)))
        return jnp.einsum('brkd,rkt->dbt', folded, time_wide)
    searched = lax.map(search, intensity.reshape(-1, beam_block_size, spec_total, CHANS))
    return searched.transpose(1, 0, 2, 3).reshape(DMS, BEAMS, spec_total)
```

```python
from functools import partial
import math

import jax
import jax.numpy as jnp
import numpy as np
from jax import lax
from jax.experimental import pallas as pl
from jax.experimental.pallas import tpu as pltpu
from jax.sharding import PartitionSpec as P

NFFT = 2048
CHANS = 1024
TAPS = 4
ROWS = 256


TWO_PI = 2.0 * math.pi
phase_modulus = 1048576


def from_behind(block, axis, distance):
    devices = range(lax.axis_size(axis))
    route = [(i - distance, i) for i in devices if i - distance in devices]
    return lax.ppermute(block, axis, route)


def pfb_window(tap_count, series_length):
    points = jnp.arange(tap_count * series_length, dtype=jnp.float32) + 0.5
    start_offset = points / series_length - tap_count / 2.0
    taper = 0.5 - 0.5 * jnp.cos(TWO_PI * points / (tap_count * series_length))
    values = (jnp.sinc(start_offset) * taper).reshape(tap_count, series_length)
    return values / jnp.sqrt(jnp.sum(values * values, axis=0, keepdims=True))


def dft_table(series_length, columns):
    product = (
        jnp.arange(series_length, dtype=jnp.int32)[:, None]
        * jnp.arange(columns, dtype=jnp.int32)[None, :]
        % series_length
    )
    angles = product.astype(jnp.float32) * (TWO_PI / series_length)
    factor = 1.0 / math.sqrt(series_length)
    return jnp.concatenate([jnp.cos(angles) * factor, -jnp.sin(angles) * factor], axis=1).astype(
        jnp.bfloat16
    )


def spectral_table(series_length):
    product = (
        jnp.arange(series_length, dtype=jnp.int32)[:, None]
        * jnp.arange(series_length, dtype=jnp.int32)[None, :]
        % series_length
    )
    angles = product.astype(jnp.float32) * (TWO_PI / series_length)
    factor = 1.0 / math.sqrt(series_length)
    nonzero = (jnp.arange(series_length) > 0)[:, None]
    cosine = jnp.where(nonzero, jnp.cos(angles) * factor, 0.0)
    sine_part = jnp.where(nonzero, -jnp.sin(angles) * factor, 0.0)
    return jnp.stack([cosine, sine_part]).astype(jnp.bfloat16)


def steer_table(coords, grid_ids, chan_ids, factor):
    phases = (
        coords[None, None, :] * grid_ids[None, :, None] * chan_ids[:, None, None] % phase_modulus
    )
    angles = phases.astype(jnp.float32) * (TWO_PI / phase_modulus)
    return (
        (jnp.cos(angles) * factor).astype(jnp.bfloat16),
        (jnp.sin(angles) * factor).astype(jnp.bfloat16),
    )


def form_beams(block_in, feed_at_grid_slot, ew_tables, ns_tables):
    ew_real, ew_imag = ew_tables
    ns_real, ns_imag = ns_tables
    item_count = block_in.shape[1]
    chan_count = block_in.shape[3]
    gridded = jnp.take(block_in, feed_at_grid_slot, axis=0).reshape(
        ROWS, 4, 2, item_count, 2, chan_count
    )
    grid_real = gridded[:, :, :, :, 0, :]
    grid_imag = gridded[:, :, :, :, 1, :]
    east_mix = partial(jnp.einsum, "cey,rypsc->erpsc", preferred_element_type=jnp.float32)
    east_real = (east_mix(ew_real, grid_real) - east_mix(ew_imag, grid_imag)).astype(jnp.bfloat16)
    east_imag = (east_mix(ew_real, grid_imag) + east_mix(ew_imag, grid_real)).astype(jnp.bfloat16)
    north_mix = partial(jnp.einsum, "cbr,erpsc->ebpsc", preferred_element_type=jnp.float32)
    beam_real = north_mix(ns_real, east_real) - north_mix(ns_imag, east_imag)
    beam_imag = north_mix(ns_real, east_imag) + north_mix(ns_imag, east_real)
    beam_power = jnp.sum(beam_real * beam_real + beam_imag * beam_imag, axis=2)
    return beam_power.reshape(-1, item_count, chan_count).astype(jnp.bfloat16)


def local_unaligned(voltages, feed_at_grid_slot, ew_grid, ns_grid, delays):
    feed_dev = voltages.shape[0]
    spec_dev = voltages.shape[1] // NFFT
    time_extent = lax.axis_size("tm")
    feed_size = lax.axis_size("feed")
    spec_total = spec_dev * time_extent
    frames = (
        (voltages.astype(jnp.float32) / 64.0).astype(jnp.bfloat16).reshape(feed_dev, spec_dev, NFFT)
    )
    history = from_behind(frames[:, spec_dev - TAPS + 1 :, :], "tm", 1)
    padded = jnp.concatenate([history, frames], axis=1)
    window = pfb_window(TAPS, NFFT)
    filtered = jnp.zeros((feed_dev, spec_dev, NFFT), jnp.float32)
    for tap_index in range(TAPS):
        filtered = filtered + window[tap_index] * padded[
            :, tap_index : tap_index + spec_dev, :
        ].astype(jnp.float32)
    spectra = jnp.dot(
        filtered.astype(jnp.bfloat16).reshape(feed_dev * spec_dev, NFFT),
        dft_table(NFFT, CHANS),
        preferred_element_type=jnp.float32,
    )
    spectra = spectra.astype(jnp.bfloat16).reshape(feed_dev, spec_dev, 2, CHANS)
    chan_dev = CHANS // feed_size
    chan_ids = lax.axis_index("feed") * chan_dev + jnp.arange(chan_dev, dtype=jnp.int32) + CHANS
    ew_tables = steer_table(jnp.arange(4, dtype=jnp.int32), ew_grid, chan_ids, 0.5)
    ns_tables = steer_table(
        jnp.arange(ROWS, dtype=jnp.int32), ns_grid, chan_ids, 1.0 / math.sqrt(ROWS)
    )
    intensity = form_beams(
        lax.all_to_all(spectra, "feed", split_axis=3, concat_axis=0, tiled=True),
        feed_at_grid_slot,
        ew_tables,
        ns_tables,
    )
    time_table = spectral_table(spec_total)
    first_freq = lax.axis_index("tm") * spec_dev
    by_beam = lax.all_to_all(intensity, "feed", split_axis=0, concat_axis=2, tiled=True)
    my_table = lax.dynamic_slice_in_dim(time_table, first_freq, spec_dev, 1)
    zero_init = jnp.zeros((by_beam.shape[0], 2, spec_dev, CHANS), jnp.float32)
    spectrum = (
        zero_init
        + jnp.einsum(
            "rkt,btc->brkc",
            my_table,
            lax.all_gather(by_beam, "tm", axis=1, tiled=True),
            preferred_element_type=jnp.float32,
        )
    ).astype(jnp.bfloat16)
    freq_ids = first_freq + jnp.arange(spec_dev, dtype=jnp.int32)
    phases = freq_ids[:, None, None] * delays[None, :, :] % spec_total
    angles = phases.astype(jnp.float32) * (TWO_PI / spec_total)
    phase_real = jnp.cos(angles).astype(jnp.bfloat16)
    phase_imag = jnp.sin(angles).astype(jnp.bfloat16)
    shift_mixture = partial(jnp.einsum, "vuw,uwt->vut", preferred_element_type=jnp.float32)
    spec_real = spectrum[:, 0]
    spec_imag = spectrum[:, 1]
    moved_real = shift_mixture(spec_real, phase_real) - shift_mixture(spec_imag, phase_imag)
    moved_imag = shift_mixture(spec_real, phase_imag) + shift_mixture(spec_imag, phase_real)
    folded = (jnp.stack([moved_real, moved_imag], axis=1) * (1.0 / math.sqrt(CHANS))).astype(
        jnp.bfloat16
    )
    combined = lax.all_to_all(folded, "tm", split_axis=3, concat_axis=2, tiled=True)
    return jnp.einsum("brkd,rkt->dbt", combined, time_table, preferred_element_type=jnp.float32)


MESH = pl.DeviceIdType.MESH


def sincos(phases, modulus):
    quarter = modulus // 4
    quadrant = (phases + quarter // 2) >> (quarter.bit_length() - 1)
    rest = (phases - quadrant * quarter).astype(jnp.float32) * (TWO_PI / modulus)
    square = rest * rest
    sine = rest * (
        1.0 + square * (-1.0 / 6 + square * (1.0 / 120 + square * (-1.0 / 5040 + square / 362880)))
    )
    cosine = 1.0 + square * (
        -0.5 + square * (1.0 / 24 + square * (-1.0 / 720 + square * (1.0 / 40320)))
    )
    swap = quadrant & 1 == 1
    first = jnp.where(swap, sine, cosine)
    second = jnp.where(swap, cosine, sine)
    turned = quadrant & 3
    return (
        jnp.where((turned == 1) | (turned == 2), -first, first),
        jnp.where(turned >= 2, -second, second),
    )


def window_constant(tap_count, series_length):
    points = np.arange(tap_count * series_length, dtype=np.float64) + 0.5
    offset = points / series_length - tap_count / 2.0
    taper = 0.5 - 0.5 * np.cos(TWO_PI * points / (tap_count * series_length))
    values = (np.sinc(offset) * taper).reshape(tap_count, series_length)
    values = values / np.sqrt(np.sum(values * values, axis=0, keepdims=True))
    return (values / 64.0).astype(np.float32)


def dft_constant(series_length, columns, blocks):
    product = np.outer(np.arange(columns), np.arange(series_length)) % series_length
    angles = product * (TWO_PI / series_length)
    factor = 1.0 / math.sqrt(series_length)
    table = np.stack([np.cos(angles) * factor, -np.sin(angles) * factor])
    table = table.reshape(2, blocks, columns // blocks, series_length).transpose(1, 0, 2, 3)
    return table.reshape(blocks, -1, series_length).astype(jnp.bfloat16)


def search_kernel(
    volt, window, twiddle, placed, steer, rot, out,
    raw, frames, hist, filtered, send, spec, placed_v, grid, east, rot_v, power, beams,
    raw_s, placed_s, rot_s, hist_ss, hist_rs, spec_ss, spec_rs, beam_ss, beam_rs,
):
    spec_dev, feed_dev, length = frames.shape
    feed_size = spec.shape[1]
    chan_dev = spec.shape[2] // 2
    tm_size = out.shape[0]
    beam_dev, ns_beams = out.shape[3], power.shape[3]
    pairs = power.shape[2]
    ews = pairs // 2
    tm = lax.axis_index("tm")
    feed = lax.axis_index("feed")
    after = lax.rem(tm + 1, tm_size)

    def other_device(step):
        other = lax.rem(tm * feed_size + feed + step, tm_size * feed_size)
        return other // feed_size, lax.rem(other, feed_size)

    barrier = pltpu.get_barrier_semaphore()

    def greet(step, _):
        pl.semaphore_signal(barrier, inc=1, device_id=other_device(step), device_id_type=MESH)
        return 0

    lax.fori_loop(1, tm_size * feed_size, greet, 0)

    def raw_copy(s):
        return pltpu.make_async_copy(
            volt.at[:, pl.ds(s * length, length)], raw.at[s % 2], raw_s.at[s % 2]
        )

    placed_copy = pltpu.make_async_copy(placed, placed_v, placed_s)
    rot_copy = pltpu.make_async_copy(rot, rot_v, rot_s)
    raw_copy(spec_dev - 1).start()
    raw_copy(spec_dev - 2).start()

    step_rows = 16

    def convert(s):
        def body(i, _):
            rows = pl.ds(pl.multiple_of(i * step_rows, step_rows), step_rows)
            frames[s, rows, :] = raw[s % 2, rows, :].astype(jnp.float32).astype(jnp.bfloat16)
            return 0

        raw_copy(s).wait()
        lax.fori_loop(0, feed_dev // step_rows, body, 0)
        if s >= 2:
            raw_copy(s - 2).start()

    def history(i):
        return pltpu.make_async_remote_copy(
            src_ref=frames.at[spec_dev - TAPS + 1 + i],
            dst_ref=hist.at[i],
            send_sem=hist_ss.at[i],
            recv_sem=hist_rs.at[i],
            device_id=(after, feed),
            device_id_type=MESH,
        )

    convert(spec_dev - 1)
    pl.semaphore_wait(barrier, tm_size * feed_size - 1)
    history(TAPS - 2).start()
    for s in range(spec_dev - 2, -1, -1):
        convert(s)
        if s >= spec_dev - TAPS + 1:
            history(s - (spec_dev - TAPS + 1)).start()
    placed_copy.start()
    rot_copy.start()

    live = jnp.where(tm > 0, 1.0, 0.0).astype(jnp.float32)

    def spec_copy(s, other, slot):
        return pltpu.make_async_remote_copy(
            src_ref=send.at[s, other],
            dst_ref=spec.at[s, slot],
            send_sem=spec_ss.at[s, other],
            recv_sem=spec_rs.at[s, slot],
            device_id=(tm, other),
            device_id_type=MESH,
        )

    def channelize(s):
        if s < TAPS - 1:
            history(s).wait_recv()

        def filter_rows(i, _):
            rows = pl.ds(pl.multiple_of(i * step_rows, step_rows), step_rows)
            total = None
            for tap in range(TAPS):
                at = s + tap - (TAPS - 1)
                weights = window[tap : tap + 1, :]
                if at < 0:
                    term = hist[TAPS - 1 + at, rows, :].astype(jnp.float32) * (weights * live)
                else:
                    term = frames[at, rows, :].astype(jnp.float32) * weights
                total = term if total is None else total + term
            filtered[rows, :] = total.astype(jnp.bfloat16)
            return 0

        lax.fori_loop(0, feed_dev // step_rows, filter_rows, 0)

        def transform(i, _):
            other = lax.rem(feed + 1 + i, feed_size)
            block = lax.dot_general(
                twiddle[other],
                filtered[...],
                (((1,), (1,)), ((), ())),
                preferred_element_type=jnp.float32,
            ).astype(jnp.bfloat16)

            @pl.when(other != feed)
            def _():
                send[s, other] = block
                spec_copy(s, other, feed).start()

            @pl.when(other == feed)
            def _():
                spec[s, other] = block

            return 0

        lax.fori_loop(0, feed_size, transform, 0)

    def arrive(s):
        def body(step, _):
            other = lax.rem(feed + step, feed_size)
            spec_copy(s, other, other).wait()
            return 0

        lax.fori_loop(1, feed_size, body, 0)

    def place(s):
        def body(m, _):
            total = jnp.zeros(grid.shape[1:], jnp.float32)
            for j in range(feed_size):
                total += jnp.dot(
                    spec[s, j],
                    placed_v[m, j * feed_dev : (j + 1) * feed_dev, :],
                    preferred_element_type=jnp.float32,
                )
            grid[m] = total
            return 0

        lax.fori_loop(0, grid.shape[0], body, 0)

    def mix_east(at):
        def body(i, _):
            start = pl.multiple_of(i * 8, 8)
            rows = pl.ds(start, 8)
            rows_im = pl.ds(pl.multiple_of(chan_dev + start, 8), 8)
            for pol in range(2):
                re = [grid[2 * y + pol, rows, :] for y in range(4)]
                im = [grid[2 * y + pol, rows_im, :] for y in range(4)]
                for e in range(ews):
                    sum_re = sum_im = None
                    for y in range(4):
                        w = e * 4 + y
                        w_re = steer[rows, w : w + 1]
                        w_im = steer[rows, 4 * ews + w : 4 * ews + w + 1]
                        term_re = w_re * re[y] - w_im * im[y]
                        term_im = w_re * im[y] + w_im * re[y]
                        sum_re = term_re if sum_re is None else sum_re + term_re
                        sum_im = term_im if sum_im is None else sum_im + term_im
                    row = at * 2 * pairs + pol * ews + e
                    east[rows, row, :] = sum_re
                    east[rows, row + pairs, :] = sum_im
            return 0

        lax.fori_loop(0, chan_dev // 8, body, 0)

    def mix_north(count):
        def body(c, _):
            coarse_re, coarse_im, fine_re, fine_im = (rot_v[k, c] for k in range(4))
            parts_re, parts_im = [], []
            for r in range(coarse_re.shape[0]):
                a_re, a_im = coarse_re[r : r + 1, :], coarse_im[r : r + 1, :]
                parts_re.append((a_re * fine_re - a_im * fine_im).astype(jnp.bfloat16))
                parts_im.append((a_re * fine_im + a_im * fine_re).astype(jnp.bfloat16))
            side = east[c, : count * 2 * pairs, :].astype(jnp.bfloat16)
            by_re = jnp.dot(
                side, jnp.concatenate(parts_re, axis=0), preferred_element_type=jnp.float32
            )
            by_im = jnp.dot(
                side, jnp.concatenate(parts_im, axis=0), preferred_element_type=jnp.float32
            )
            for k in range(count):
                lo, mid, hi = 2 * k * pairs, (2 * k + 1) * pairs, (2 * k + 2) * pairs
                beam_re = by_re[lo:mid] - by_im[mid:hi]
                beam_im = by_re[mid:hi] + by_im[lo:mid]
                power[k, c] = beam_re * beam_re + beam_im * beam_im
            return 0

        lax.fori_loop(0, chan_dev, body, 0)

    def transpose_power(s, k):
        width = beam_dev * tm_size
        for e in range(ews):
            total = power[k, :, e, :] + power[k, :, ews + e, :]
            turned = total.T.astype(jnp.bfloat16)
            for part in range(ns_beams // beam_dev):
                first = e * ns_beams + part * beam_dev
                block = turned[part * beam_dev : (part + 1) * beam_dev]
                beams[first % width // beam_dev, first // width, s] = block

    def beam_copy(first, last, group, peer, slot):
        return pltpu.make_async_remote_copy(
            src_ref=beams.at[peer[0], peer[1], pl.ds(first, last - first)],
            dst_ref=out.at[slot[0], slot[1], pl.ds(first, last - first)],
            send_sem=beam_ss.at[group, peer[0], peer[1]],
            recv_sem=beam_rs.at[group, slot[0], slot[1]],
            device_id=peer,
            device_id_type=MESH,
        )

    groups = [(spec_dev - 1, 1), (0, 0)] if spec_dev > 1 else [(0, 0)]

    def form(group):
        high, low = groups[group]
        for k, s in enumerate(range(low, high + 1)):
            place(s)
            mix_east(k)
        mix_north(high + 1 - low)
        for k, s in enumerate(range(low, high + 1)):
            transpose_power(s, k)

        def go(step, _):
            beam_copy(low, high + 1, group, other_device(step), (tm, feed)).start()
            return 0

        lax.fori_loop(1, tm_size * feed_size, go, 0)
        out[tm, feed, low : high + 1] = beams[tm, feed, low : high + 1]

    for s in range(spec_dev - 1, -1, -1):
        channelize(s)
    placed_copy.wait()
    rot_copy.wait()
    for group, (high, low) in enumerate(groups):
        for s in range(high, low - 1, -1):
            arrive(s)
        form(group)
    for group, (high, low) in enumerate(groups):
        def finish(step, _):
            peer = other_device(step)
            beam_copy(low, high + 1, group, peer, peer).wait()
            return 0

        lax.fori_loop(1, tm_size * feed_size, finish, 0)
    for i in range(TAPS - 1):
        history(i).wait_send()


def search(voltages, placed, steer, rot, tm_size, feed_size, beam_dev):
    feed_dev = voltages.shape[0]
    spec_dev = voltages.shape[1] // NFFT
    chan_dev = CHANS // feed_size
    ns_beams = rot.shape[3]
    pairs = 2 * steer.shape[1] // 8
    window = jnp.asarray(window_constant(TAPS, NFFT))
    twiddle = jnp.asarray(dft_constant(NFFT, CHANS, feed_size))
    blocks = (spec_dev, feed_size, 2 * chan_dev, feed_dev)
    batch = max(spec_dev - 1, 1)
    vmem = pl.BlockSpec(memory_space=pltpu.VMEM)
    hbm = pl.BlockSpec(memory_space=pl.ANY)
    dma = pltpu.SemaphoreType.DMA
    sent = (tm_size, feed_size, spec_dev, beam_dev, chan_dev)
    return pl.pallas_call(
        search_kernel,
        out_shape=jax.ShapeDtypeStruct(sent, jnp.bfloat16),
        in_specs=[hbm, vmem, vmem, hbm, vmem, hbm],
        out_specs=vmem,
        scratch_shapes=[
            pltpu.VMEM((2, feed_dev, NFFT), jnp.int32),
            pltpu.VMEM((spec_dev, feed_dev, NFFT), jnp.bfloat16),
            pltpu.VMEM((TAPS - 1, feed_dev, NFFT), jnp.bfloat16),
            pltpu.VMEM((feed_dev, NFFT), jnp.bfloat16),
            pltpu.VMEM(blocks, jnp.bfloat16),
            pltpu.VMEM(blocks, jnp.bfloat16),
            pltpu.VMEM(placed.shape, jnp.bfloat16),
            pltpu.VMEM((placed.shape[0], 2 * chan_dev, placed.shape[2]), jnp.float32),
            pltpu.VMEM((chan_dev, batch * 2 * pairs, ROWS), jnp.float32),
            pltpu.VMEM(rot.shape, jnp.float32),
            pltpu.VMEM((batch, chan_dev, pairs, ns_beams), jnp.float32),
            pltpu.VMEM(sent, jnp.bfloat16),
            dma((2,)),
            dma(()),
            dma(()),
            dma((TAPS - 1,)),
            dma((TAPS - 1,)),
            dma((spec_dev, feed_size)),
            dma((spec_dev, feed_size)),
            dma((2, tm_size, feed_size)),
            dma((2, tm_size, feed_size)),
        ],
        compiler_params=pltpu.CompilerParams(
            collective_id=0, has_side_effects=True, vmem_limit_bytes=60 * 1024 * 1024
        ),
        name="search",
    )(voltages, window, twiddle, placed, steer, rot)


def ns_rotations(ns_grid, chan_ids, stride):
    coarse = jnp.arange(ROWS // stride, dtype=jnp.int32) * stride
    fine = jnp.arange(stride, dtype=jnp.int32)
    step = (ns_grid[None, :] * chan_ids[:, None]) & (phase_modulus - 1)
    tables = []
    for rows in (coarse, fine):
        phases = (rows[None, :, None] * step[:, None, :]) & (phase_modulus - 1)
        tables.append(sincos(phases, phase_modulus))
    return tables


def local(voltages, feed_at_grid_slot, ew_grid, ns_grid, delays):
    spec_dev = voltages.shape[1] // NFFT
    tm_size = lax.axis_size("tm")
    feed_size = lax.axis_size("feed")
    spec_total = spec_dev * tm_size
    chan_dev = CHANS // feed_size
    feeds = feed_at_grid_slot.shape[0]

    slots = feed_at_grid_slot.reshape(ROWS, 8).T
    placed = jnp.arange(feeds, dtype=jnp.int32)[None, :, None] == slots[:, None, :]
    placed = placed.astype(jnp.bfloat16)

    chan_ids = lax.axis_index("feed") * chan_dev + jnp.arange(chan_dev, dtype=jnp.int32) + CHANS
    phases = (
        jnp.arange(4, dtype=jnp.int32)[None, None, :]
        * ew_grid[None, :, None]
        * chan_ids[:, None, None]
    ) & (phase_modulus - 1)
    ew = [part.reshape(chan_dev, -1) * 0.5 for part in sincos(phases, phase_modulus)]
    steer = jnp.concatenate(ew, axis=1).astype(jnp.bfloat16).astype(jnp.float32)

    coarse, fine = ns_rotations(ns_grid, chan_ids, 16)
    factor = 1.0 / math.sqrt(ROWS)
    rot = jnp.stack([coarse[0] * factor, coarse[1] * factor, fine[0], fine[1]])

    beam_dev = ew_grid.shape[0] * ns_grid.shape[0] // (tm_size * feed_size)
    blocks = search(voltages, placed, steer, rot, tm_size, feed_size, beam_dev)
    by_beam = blocks.transpose(0, 2, 3, 1, 4).reshape(spec_total, beam_dev, CHANS)

    half = spec_total // 2
    factor = 1.0 / math.sqrt(spec_total)
    freq_ids = np.arange(1, half + 1)
    turn = np.outer(freq_ids, np.arange(spec_total)) % spec_total * (TWO_PI / spec_total)
    table = np.stack([np.cos(turn), -np.sin(turn)]) * factor
    time_table = jnp.asarray(table.astype(jnp.bfloat16))
    spectrum = jnp.einsum("rkt,tbc->krbc", time_table, by_beam, preferred_element_type=jnp.float32)
    spectrum = spectrum.astype(jnp.bfloat16).reshape(half, 2 * beam_dev, CHANS)
    base_re, base_im = sincos(delays & (spec_total - 1), spec_total)
    powers_re, powers_im = [base_re], [base_im]
    for _ in range(1, half):
        re, im = powers_re[-1], powers_im[-1]
        powers_re.append(re * base_re - im * base_im)
        powers_im.append(re * base_im + im * base_re)
    phase = jnp.stack([jnp.stack(powers_re), jnp.stack(powers_im)], axis=2).astype(jnp.bfloat16)
    phase = phase.reshape(half, CHANS, -1)
    moved = jnp.einsum("kmc,kcd->kmd", spectrum, phase, preferred_element_type=jnp.float32)
    moved = moved.reshape(half, 2, beam_dev, 2, -1)
    moved_real = moved[:, 0, :, 0] - moved[:, 1, :, 1]
    moved_imag = moved[:, 0, :, 1] + moved[:, 1, :, 0]
    folded = jnp.stack([moved_real, moved_imag]) * (1.0 / math.sqrt(CHANS))
    folded = folded.astype(jnp.bfloat16)
    combined = lax.all_to_all(folded, "tm", split_axis=3, concat_axis=2, tiled=True)
    weight = np.where(2 * freq_ids == spec_total, 1.0, 2.0)[None, :, None]
    back = jnp.asarray((table.astype(jnp.bfloat16).astype(np.float64) * weight).astype(jnp.bfloat16))
    return jnp.einsum("rkbd,rkt->dbt", combined, back, preferred_element_type=jnp.float32)


def solution(mesh):
    in_specs = (P("feed", "tm"), P(), P(), P(), P())
    out_specs = P("tm", "feed", None)
    aligned = CHANS // mesh.shape["feed"] % 128 == 0
    body = local if aligned else local_unaligned
    return jax.shard_map(body, mesh=mesh, in_specs=in_specs, out_specs=out_specs, check_vma=False)
```

```python
from functools import partial
import math

import jax
import jax.numpy as jnp
import numpy as np
from jax import lax
from jax.experimental import pallas as pl
from jax.experimental.pallas import tpu as pltpu
from jax.sharding import PartitionSpec as P

NFFT = 2048
CHANS = 1024
TAPS = 4
ROWS = 256


TWO_PI = 2.0 * math.pi
phase_modulus = 1048576


def from_behind(block, axis, distance):
    devices = range(lax.axis_size(axis))
    route = [(i - distance, i) for i in devices if i - distance in devices]
    return lax.ppermute(block, axis, route)


def pfb_window(tap_count, series_length):
    points = jnp.arange(tap_count * series_length, dtype=jnp.float32) + 0.5
    start_offset = points / series_length - tap_count / 2.0
    taper = 0.5 - 0.5 * jnp.cos(TWO_PI * points / (tap_count * series_length))
    values = (jnp.sinc(start_offset) * taper).reshape(tap_count, series_length)
    return values / jnp.sqrt(jnp.sum(values * values, axis=0, keepdims=True))


def dft_table(series_length, columns):
    product = (
        jnp.arange(series_length, dtype=jnp.int32)[:, None]
        * jnp.arange(columns, dtype=jnp.int32)[None, :]
        % series_length
    )
    angles = product.astype(jnp.float32) * (TWO_PI / series_length)
    factor = 1.0 / math.sqrt(series_length)
    return jnp.concatenate([jnp.cos(angles) * factor, -jnp.sin(angles) * factor], axis=1).astype(
        jnp.bfloat16
    )


def spectral_table(series_length):
    product = (
        jnp.arange(series_length, dtype=jnp.int32)[:, None]
        * jnp.arange(series_length, dtype=jnp.int32)[None, :]
        % series_length
    )
    angles = product.astype(jnp.float32) * (TWO_PI / series_length)
    factor = 1.0 / math.sqrt(series_length)
    nonzero = (jnp.arange(series_length) > 0)[:, None]
    cosine = jnp.where(nonzero, jnp.cos(angles) * factor, 0.0)
    sine_part = jnp.where(nonzero, -jnp.sin(angles) * factor, 0.0)
    return jnp.stack([cosine, sine_part]).astype(jnp.bfloat16)


def steer_table(coords, grid_ids, chan_ids, factor):
    phases = (
        coords[None, None, :] * grid_ids[None, :, None] * chan_ids[:, None, None] % phase_modulus
    )
    angles = phases.astype(jnp.float32) * (TWO_PI / phase_modulus)
    return (
        (jnp.cos(angles) * factor).astype(jnp.bfloat16),
        (jnp.sin(angles) * factor).astype(jnp.bfloat16),
    )


def form_beams(block_in, feed_at_grid_slot, ew_tables, ns_tables):
    ew_real, ew_imag = ew_tables
    ns_real, ns_imag = ns_tables
    item_count = block_in.shape[1]
    chan_count = block_in.shape[3]
    gridded = jnp.take(block_in, feed_at_grid_slot, axis=0).reshape(
        ROWS, 4, 2, item_count, 2, chan_count
    )
    grid_real = gridded[:, :, :, :, 0, :]
    grid_imag = gridded[:, :, :, :, 1, :]
    east_mix = partial(jnp.einsum, "cey,rypsc->erpsc", preferred_element_type=jnp.float32)
    east_real = (east_mix(ew_real, grid_real) - east_mix(ew_imag, grid_imag)).astype(jnp.bfloat16)
    east_imag = (east_mix(ew_real, grid_imag) + east_mix(ew_imag, grid_real)).astype(jnp.bfloat16)
    north_mix = partial(jnp.einsum, "cbr,erpsc->ebpsc", preferred_element_type=jnp.float32)
    beam_real = north_mix(ns_real, east_real) - north_mix(ns_imag, east_imag)
    beam_imag = north_mix(ns_real, east_imag) + north_mix(ns_imag, east_real)
    beam_power = jnp.sum(beam_real * beam_real + beam_imag * beam_imag, axis=2)
    return beam_power.reshape(-1, item_count, chan_count).astype(jnp.bfloat16)


def local_unaligned(voltages, feed_at_grid_slot, ew_grid, ns_grid, delays):
    feed_dev = voltages.shape[0]
    spec_dev = voltages.shape[1] // NFFT
    time_extent = lax.axis_size("tm")
    feed_size = lax.axis_size("feed")
    spec_total = spec_dev * time_extent
    frames = (
        (voltages.astype(jnp.float32) / 64.0).astype(jnp.bfloat16).reshape(feed_dev, spec_dev, NFFT)
    )
    history = from_behind(frames[:, spec_dev - TAPS + 1 :, :], "tm", 1)
    padded = jnp.concatenate([history, frames], axis=1)
    window = pfb_window(TAPS, NFFT)
    filtered = jnp.zeros((feed_dev, spec_dev, NFFT), jnp.float32)
    for tap_index in range(TAPS):
        filtered = filtered + window[tap_index] * padded[
            :, tap_index : tap_index + spec_dev, :
        ].astype(jnp.float32)
    spectra = jnp.dot(
        filtered.astype(jnp.bfloat16).reshape(feed_dev * spec_dev, NFFT),
        dft_table(NFFT, CHANS),
        preferred_element_type=jnp.float32,
    )
    spectra = spectra.astype(jnp.bfloat16).reshape(feed_dev, spec_dev, 2, CHANS)
    chan_dev = CHANS // feed_size
    chan_ids = lax.axis_index("feed") * chan_dev + jnp.arange(chan_dev, dtype=jnp.int32) + CHANS
    ew_tables = steer_table(jnp.arange(4, dtype=jnp.int32), ew_grid, chan_ids, 0.5)
    ns_tables = steer_table(
        jnp.arange(ROWS, dtype=jnp.int32), ns_grid, chan_ids, 1.0 / math.sqrt(ROWS)
    )
    intensity = form_beams(
        lax.all_to_all(spectra, "feed", split_axis=3, concat_axis=0, tiled=True),
        feed_at_grid_slot,
        ew_tables,
        ns_tables,
    )
    time_table = spectral_table(spec_total)
    first_freq = lax.axis_index("tm") * spec_dev
    by_beam = lax.all_to_all(intensity, "feed", split_axis=0, concat_axis=2, tiled=True)
    my_table = lax.dynamic_slice_in_dim(time_table, first_freq, spec_dev, 1)
    zero_init = jnp.zeros((by_beam.shape[0], 2, spec_dev, CHANS), jnp.float32)
    spectrum = (
        zero_init
        + jnp.einsum(
            "rkt,btc->brkc",
            my_table,
            lax.all_gather(by_beam, "tm", axis=1, tiled=True),
            preferred_element_type=jnp.float32,
        )
    ).astype(jnp.bfloat16)
    freq_ids = first_freq + jnp.arange(spec_dev, dtype=jnp.int32)
    phases = freq_ids[:, None, None] * delays[None, :, :] % spec_total
    angles = phases.astype(jnp.float32) * (TWO_PI / spec_total)
    phase_real = jnp.cos(angles).astype(jnp.bfloat16)
    phase_imag = jnp.sin(angles).astype(jnp.bfloat16)
    shift_mixture = partial(jnp.einsum, "vuw,uwt->vut", preferred_element_type=jnp.float32)
    spec_real = spectrum[:, 0]
    spec_imag = spectrum[:, 1]
    moved_real = shift_mixture(spec_real, phase_real) - shift_mixture(spec_imag, phase_imag)
    moved_imag = shift_mixture(spec_real, phase_imag) + shift_mixture(spec_imag, phase_real)
    folded = (jnp.stack([moved_real, moved_imag], axis=1) * (1.0 / math.sqrt(CHANS))).astype(
        jnp.bfloat16
    )
    combined = lax.all_to_all(folded, "tm", split_axis=3, concat_axis=2, tiled=True)
    return jnp.einsum("brkd,rkt->dbt", combined, time_table, preferred_element_type=jnp.float32)


MESH = pl.DeviceIdType.MESH


def sincos(phases, modulus):
    quarter = modulus // 4
    quadrant = (phases + quarter // 2) >> (quarter.bit_length() - 1)
    rest = (phases - quadrant * quarter).astype(jnp.float32) * (TWO_PI / modulus)
    square = rest * rest
    sine = rest * (
        1.0 + square * (-1.0 / 6 + square * (1.0 / 120 + square * (-1.0 / 5040 + square / 362880)))
    )
    cosine = 1.0 + square * (
        -0.5 + square * (1.0 / 24 + square * (-1.0 / 720 + square * (1.0 / 40320)))
    )
    swap = quadrant & 1 == 1
    first = jnp.where(swap, sine, cosine)
    second = jnp.where(swap, cosine, sine)
    turned = quadrant & 3
    return (
        jnp.where((turned == 1) | (turned == 2), -first, first),
        jnp.where(turned >= 2, -second, second),
    )


def window_constant(tap_count, series_length):
    points = np.arange(tap_count * series_length, dtype=np.float64) + 0.5
    offset = points / series_length - tap_count / 2.0
    taper = 0.5 - 0.5 * np.cos(TWO_PI * points / (tap_count * series_length))
    values = (np.sinc(offset) * taper).reshape(tap_count, series_length)
    values = values / np.sqrt(np.sum(values * values, axis=0, keepdims=True))
    return (values / 64.0).astype(np.float32)


def dft_constant(series_length, columns, blocks):
    product = np.outer(np.arange(columns), np.arange(series_length)) % series_length
    angles = product * (TWO_PI / series_length)
    factor = 1.0 / math.sqrt(series_length)
    table = np.stack([np.cos(angles) * factor, -np.sin(angles) * factor])
    table = table.reshape(2, blocks, columns // blocks, series_length).transpose(1, 0, 2, 3)
    return table.reshape(blocks, -1, series_length).astype(jnp.bfloat16)


def search_kernel(
    volt, window, twiddle_hbm, slots, ew_row, ns_row, out,
    raw, frames, hist, filtered, send, spec, twiddle, placed_v, grid, east, steer, rot_v, power,
    beams, raw_s, twiddle_s, hist_ss, hist_rs, spec_ss, spec_rs, beam_ss, beam_rs,
):
    spec_dev, feed_dev, length = frames.shape
    feed_size = spec.shape[1]
    chan_dev = spec.shape[2] // 2
    tm_size = out.shape[0]
    beam_dev, ns_beams = out.shape[3], power.shape[3]
    pairs = power.shape[2]
    ews = pairs // 2
    tm = lax.axis_index("tm")
    feed = lax.axis_index("feed")
    after = lax.rem(tm + 1, tm_size)

    def other_device(step):
        other = lax.rem(tm * feed_size + feed + step, tm_size * feed_size)
        return other // feed_size, lax.rem(other, feed_size)

    barrier = pltpu.get_barrier_semaphore()

    def greet(step, _):
        pl.semaphore_signal(barrier, inc=1, device_id=other_device(step), device_id_type=MESH)
        return 0

    lax.fori_loop(1, tm_size * feed_size, greet, 0)

    def raw_copy(s):
        return pltpu.make_async_copy(
            volt.at[:, pl.ds(s * length, length)], raw.at[s % 2], raw_s.at[s % 2]
        )

    twiddle_copy = pltpu.make_async_copy(twiddle_hbm, twiddle, twiddle_s)
    raw_copy(spec_dev - 1).start()
    raw_copy(spec_dev - 2).start()
    twiddle_copy.start()

    step_rows = 16

    def convert(s):
        def body(i, _):
            rows = pl.ds(pl.multiple_of(i * step_rows, step_rows), step_rows)
            frames[s, rows, :] = raw[s % 2, rows, :].astype(jnp.float32).astype(jnp.bfloat16)
            return 0

        raw_copy(s).wait()
        lax.fori_loop(0, feed_dev // step_rows, body, 0)
        if s >= 2:
            raw_copy(s - 2).start()

    def history(i):
        return pltpu.make_async_remote_copy(
            src_ref=frames.at[spec_dev - TAPS + 1 + i],
            dst_ref=hist.at[i],
            send_sem=hist_ss.at[i],
            recv_sem=hist_rs.at[i],
            device_id=(after, feed),
            device_id_type=MESH,
        )

    convert(spec_dev - 1)
    pl.semaphore_wait(barrier, tm_size * feed_size - 1)
    history(TAPS - 2).start()
    for s in range(spec_dev - 2, -1, -1):
        convert(s)
        if s >= spec_dev - TAPS + 1:
            history(s - (spec_dev - TAPS + 1)).start()
    twiddle_copy.wait()

    live = jnp.where(tm > 0, 1.0, 0.0).astype(jnp.float32)

    def spec_copy(s, other, slot):
        return pltpu.make_async_remote_copy(
            src_ref=send.at[s, other],
            dst_ref=spec.at[s, slot],
            send_sem=spec_ss.at[s, other],
            recv_sem=spec_rs.at[s, slot],
            device_id=(tm, other),
            device_id_type=MESH,
        )

    def channelize(s):
        if s < TAPS - 1:
            history(s).wait_recv()

        def filter_rows(i, _):
            rows = pl.ds(pl.multiple_of(i * step_rows, step_rows), step_rows)
            total = None
            for tap in range(TAPS):
                at = s + tap - (TAPS - 1)
                weights = window[tap : tap + 1, :]
                if at < 0:
                    term = hist[TAPS - 1 + at, rows, :].astype(jnp.float32) * (weights * live)
                else:
                    term = frames[at, rows, :].astype(jnp.float32) * weights
                total = term if total is None else total + term
            filtered[rows, :] = total.astype(jnp.bfloat16)
            return 0

        lax.fori_loop(0, feed_dev // step_rows, filter_rows, 0)

        def transform(i, _):
            other = lax.rem(feed + 1 + i, feed_size)
            block = lax.dot_general(
                twiddle[other],
                filtered[...],
                (((1,), (1,)), ((), ())),
                preferred_element_type=jnp.float32,
            ).astype(jnp.bfloat16)

            @pl.when(other != feed)
            def _():
                send[s, other] = block
                spec_copy(s, other, feed).start()

            @pl.when(other == feed)
            def _():
                spec[s, other] = block

            return 0

        lax.fori_loop(0, feed_size, transform, 0)

    def make_tables():
        def one_hot(i, _):
            rows = pl.ds(pl.multiple_of(i * step_rows, step_rows), step_rows)
            shape = (step_rows, placed_v.shape[2])
            feeds = lax.broadcasted_iota(jnp.int32, shape, 0) + i * step_rows
            for m in range(placed_v.shape[0]):
                hit = feeds == slots[m : m + 1, :]
                placed_v[m, rows, :] = jnp.where(hit, 1.0, 0.0).astype(jnp.bfloat16)
            return 0

        lax.fori_loop(0, placed_v.shape[1] // step_rows, one_hot, 0)
        first = feed * chan_dev + CHANS
        chans = lax.broadcasted_iota(jnp.int32, (chan_dev, 4 * ews), 0) + first
        turns = sincos((ew_row[...] * chans) & (phase_modulus - 1), phase_modulus)
        for part, value in enumerate(turns):
            value = (value * 0.5).astype(jnp.bfloat16).astype(jnp.float32)
            steer[:, part * 4 * ews : (part + 1) * 4 * ews] = value
        fine_rows = rot_v.shape[2]
        row_ids = lax.broadcasted_iota(jnp.int32, (fine_rows, ns_beams), 0)
        factor = 1.0 / math.sqrt(ROWS)

        def rotations(c, _):
            phases = row_ids * ((ns_row[...] * (first + c)) & (phase_modulus - 1))
            fine = sincos(phases & (phase_modulus - 1), phase_modulus)
            coarse = sincos((phases * fine_rows) & (phase_modulus - 1), phase_modulus)
            rot_v[0, c] = coarse[0] * factor
            rot_v[1, c] = coarse[1] * factor
            rot_v[2, c] = fine[0]
            rot_v[3, c] = fine[1]
            return 0

        lax.fori_loop(0, chan_dev, rotations, 0)

    def arrive(s):
        def body(step, _):
            other = lax.rem(feed + step, feed_size)
            spec_copy(s, other, other).wait()
            return 0

        lax.fori_loop(1, feed_size, body, 0)

    def place(s):
        def body(m, _):
            total = jnp.zeros(grid.shape[1:], jnp.float32)
            for j in range(feed_size):
                total += jnp.dot(
                    spec[s, j],
                    placed_v[m, j * feed_dev : (j + 1) * feed_dev, :],
                    preferred_element_type=jnp.float32,
                )
            grid[m] = total
            return 0

        lax.fori_loop(0, grid.shape[0], body, 0)

    def mix_east(at):
        def body(i, _):
            start = pl.multiple_of(i * 8, 8)
            rows = pl.ds(start, 8)
            rows_im = pl.ds(pl.multiple_of(chan_dev + start, 8), 8)
            for pol in range(2):
                re = [grid[2 * y + pol, rows, :] for y in range(4)]
                im = [grid[2 * y + pol, rows_im, :] for y in range(4)]
                for e in range(ews):
                    sum_re = sum_im = None
                    for y in range(4):
                        w = e * 4 + y
                        w_re = steer[rows, w : w + 1]
                        w_im = steer[rows, 4 * ews + w : 4 * ews + w + 1]
                        term_re = w_re * re[y] - w_im * im[y]
                        term_im = w_re * im[y] + w_im * re[y]
                        sum_re = term_re if sum_re is None else sum_re + term_re
                        sum_im = term_im if sum_im is None else sum_im + term_im
                    row = at * 2 * pairs + pol * ews + e
                    east[rows, row, :] = sum_re
                    east[rows, row + pairs, :] = sum_im
            return 0

        lax.fori_loop(0, chan_dev // 8, body, 0)

    def mix_north(count):
        def channel(c):
            coarse_re, coarse_im, fine_re, fine_im = (rot_v[k, c] for k in range(4))
            parts_re, parts_im = [], []
            for r in range(coarse_re.shape[0]):
                a_re, a_im = coarse_re[r : r + 1, :], coarse_im[r : r + 1, :]
                parts_re.append((a_re * fine_re - a_im * fine_im).astype(jnp.bfloat16))
                parts_im.append((a_re * fine_im + a_im * fine_re).astype(jnp.bfloat16))
            side = east[c, : count * 2 * pairs, :].astype(jnp.bfloat16)
            by_re = jnp.dot(
                side, jnp.concatenate(parts_re, axis=0), preferred_element_type=jnp.float32
            )
            by_im = jnp.dot(
                side, jnp.concatenate(parts_im, axis=0), preferred_element_type=jnp.float32
            )
            for k in range(count):
                lo, mid, hi = 2 * k * pairs, (2 * k + 1) * pairs, (2 * k + 2) * pairs
                beam_re = by_re[lo:mid] - by_im[mid:hi]
                beam_im = by_re[mid:hi] + by_im[lo:mid]
                power[k, c] = beam_re * beam_re + beam_im * beam_im

        def body(i, _):
            for c in range(4):
                channel(i * 4 + c)
            return 0

        lax.fori_loop(0, chan_dev // 4, body, 0)

    def transpose_power(s, k):
        width = beam_dev * tm_size
        for e in range(ews):
            total = power[k, :, e, :] + power[k, :, ews + e, :]
            turned = total.T.astype(jnp.bfloat16)
            for part in range(ns_beams // beam_dev):
                first = e * ns_beams + part * beam_dev
                block = turned[part * beam_dev : (part + 1) * beam_dev]
                beams[first % width // beam_dev, first // width, s] = block

    def beam_copy(first, last, group, peer, slot):
        return pltpu.make_async_remote_copy(
            src_ref=beams.at[peer[0], peer[1], pl.ds(first, last - first)],
            dst_ref=out.at[slot[0], slot[1], pl.ds(first, last - first)],
            send_sem=beam_ss.at[group, peer[0], peer[1]],
            recv_sem=beam_rs.at[group, slot[0], slot[1]],
            device_id=peer,
            device_id_type=MESH,
        )

    groups = [(s, s) for s in range(min(spec_dev, 2) - 1, -1, -1)]
    if spec_dev > 2:
        groups = [(spec_dev - 1, 2)] + groups

    def form(group):
        high, low = groups[group]
        mix_north(high + 1 - low)
        for k, s in enumerate(range(low, high + 1)):
            transpose_power(s, k)

        def go(step, _):
            beam_copy(low, high + 1, group, other_device(step), (tm, feed)).start()
            return 0

        lax.fori_loop(1, tm_size * feed_size, go, 0)
        out[tm, feed, low : high + 1] = beams[tm, feed, low : high + 1]

    def beamform(s):
        for group, (high, low) in enumerate(groups):
            if low <= s <= high:
                arrive(s)
                place(s)
                mix_east(s - low)
                if s == low:
                    form(group)

    channelize(spec_dev - 1)
    make_tables()
    for s in range(spec_dev - 2, -1, -1):
        channelize(s)
        beamform(s + 1)
    beamform(0)
    for group, (high, low) in enumerate(groups):
        def finish(step, _):
            peer = other_device(step)
            beam_copy(low, high + 1, group, peer, peer).wait()
            return 0

        lax.fori_loop(1, tm_size * feed_size, finish, 0)
    for i in range(TAPS - 1):
        history(i).wait_send()


def search(voltages, slots, ew_row, ns_row, tm_size, feed_size, beam_dev):
    feed_dev = voltages.shape[0]
    spec_dev = voltages.shape[1] // NFFT
    chan_dev = CHANS // feed_size
    ns_beams = ns_row.shape[1]
    pairs = 2 * ew_row.shape[1] // 4
    fine_rows = math.isqrt(ROWS)
    window = jnp.asarray(window_constant(TAPS, NFFT))
    twiddle = jnp.asarray(dft_constant(NFFT, CHANS, feed_size))
    blocks = (spec_dev, feed_size, 2 * chan_dev, feed_dev)
    batch = max(spec_dev - 2, 1)
    vmem = pl.BlockSpec(memory_space=pltpu.VMEM)
    hbm = pl.BlockSpec(memory_space=pl.ANY)
    dma = pltpu.SemaphoreType.DMA
    sent = (tm_size, feed_size, spec_dev, beam_dev, chan_dev)
    return pl.pallas_call(
        search_kernel,
        out_shape=jax.ShapeDtypeStruct(sent, jnp.bfloat16),
        in_specs=[hbm, vmem, hbm, vmem, vmem, vmem],
        out_specs=vmem,
        scratch_shapes=[
            pltpu.VMEM((2, feed_dev, NFFT), jnp.int32),
            pltpu.VMEM((spec_dev, feed_dev, NFFT), jnp.bfloat16),
            pltpu.VMEM((TAPS - 1, feed_dev, NFFT), jnp.bfloat16),
            pltpu.VMEM((feed_dev, NFFT), jnp.bfloat16),
            pltpu.VMEM(blocks, jnp.bfloat16),
            pltpu.VMEM(blocks, jnp.bfloat16),
            pltpu.VMEM(twiddle.shape, jnp.bfloat16),
            pltpu.VMEM((slots.shape[0], slots.size, ROWS), jnp.bfloat16),
            pltpu.VMEM((slots.shape[0], 2 * chan_dev, ROWS), jnp.float32),
            pltpu.VMEM((chan_dev, batch * 2 * pairs, ROWS), jnp.float32),
            pltpu.VMEM((chan_dev, 2 * ew_row.shape[1]), jnp.float32),
            pltpu.VMEM((4, chan_dev, fine_rows, ns_beams), jnp.float32),
            pltpu.VMEM((batch, chan_dev, pairs, ns_beams), jnp.float32),
            pltpu.VMEM(sent, jnp.bfloat16),
            dma((2,)),
            dma(()),
            dma((TAPS - 1,)),
            dma((TAPS - 1,)),
            dma((spec_dev, feed_size)),
            dma((spec_dev, feed_size)),
            dma((3, tm_size, feed_size)),
            dma((3, tm_size, feed_size)),
        ],
        compiler_params=pltpu.CompilerParams(
            collective_id=0, has_side_effects=True, vmem_limit_bytes=60 * 1024 * 1024
        ),
        name="search",
    )(voltages, window, twiddle, slots, ew_row, ns_row)


def transform_table(spec_total):
    ids = np.outer(np.arange(1, spec_total // 2 + 1), np.arange(spec_total)) % spec_total
    turn = ids * (TWO_PI / spec_total)
    table = np.stack([np.cos(turn), -np.sin(turn)]) / math.sqrt(spec_total)
    return table.astype(jnp.bfloat16).astype(np.float64)


def dedisperse_kernel(series, delays, out, freq, phase, send, recv, result, send_s, recv_s):
    tm_size, feed_size, spec_dev, beam_dev, chan_dev = series.shape
    spec_total = spec_dev * tm_size
    half = spec_total // 2
    trials = delays.shape[1]
    trial_dev = trials // tm_size
    table = transform_table(spec_total)
    tm = lax.axis_index("tm")
    feed = lax.axis_index("feed")

    barrier = pltpu.get_barrier_semaphore()
    for step in range(1, tm_size):
        other = lax.rem(tm + step, tm_size)
        pl.semaphore_signal(barrier, inc=1, device_id=(other, feed), device_id_type=MESH)

    def to_frequency(f, _):
        lanes = pl.ds(pl.multiple_of(f * chan_dev, chan_dev), chan_dev)
        x = [
            series[t // spec_dev, f, t % spec_dev].astype(jnp.float32) for t in range(spec_total)
        ]
        even = [x[t] + x[spec_total - t] for t in range(1, half)]
        odd = [x[t] - x[spec_total - t] for t in range(1, half)]
        for k in range(half):
            re = x[0] * float(table[0, k, 0]) + x[half] * float(table[0, k, half])
            im = None
            for t in range(1, half):
                re = re + even[t - 1] * float(table[0, k, t])
                term = odd[t - 1] * float(table[1, k, t])
                im = term if im is None else im + term
            freq[k, :beam_dev, lanes] = re.astype(jnp.bfloat16)
            freq[k, beam_dev:, lanes] = im.astype(jnp.bfloat16)
        return 0

    lax.fori_loop(0, feed_size, to_frequency, 0)

    step_rows = 16

    def make_phase(i, _):
        rows = pl.ds(pl.multiple_of(i * step_rows, step_rows), step_rows)
        base_re, base_im = sincos(delays[rows, :] & (spec_total - 1), spec_total)
        re, im = base_re, base_im
        for k in range(half):
            phase[k, rows, :trials] = re.astype(jnp.bfloat16)
            phase[k, rows, trials:] = im.astype(jnp.bfloat16)
            re, im = re * base_re - im * base_im, re * base_im + im * base_re
        return 0

    lax.fori_loop(0, delays.shape[0] // step_rows, make_phase, 0)

    def move(k, _):
        mixed = jnp.dot(freq[k], phase[k], preferred_element_type=jnp.float32)
        factor = 1.0 / math.sqrt(CHANS)
        re = (mixed[:beam_dev, :trials] - mixed[beam_dev:, trials:]) * factor
        im = (mixed[:beam_dev, trials:] + mixed[beam_dev:, :trials]) * factor
        for u in range(tm_size):
            part = slice(u * trial_dev, (u + 1) * trial_dev)
            send[u, k] = re[:, part].astype(jnp.bfloat16)
            send[u, half + k] = im[:, part].astype(jnp.bfloat16)
        return 0

    lax.fori_loop(0, half, move, 0)

    def exchange(other, slot):
        return pltpu.make_async_remote_copy(
            src_ref=send.at[other],
            dst_ref=recv.at[slot],
            send_sem=send_s.at[other],
            recv_sem=recv_s.at[slot],
            device_id=(other, feed),
            device_id_type=MESH,
        )

    pl.semaphore_wait(barrier, tm_size - 1)
    for step in range(1, tm_size):
        exchange(lax.rem(tm + step, tm_size), tm).start()
    recv[tm] = send[tm]
    for step in range(1, tm_size):
        other = lax.rem(tm + step, tm_size)
        exchange(other, other).wait()

    def to_time(u, _):
        rows = pl.ds(pl.multiple_of(u * beam_dev, beam_dev), beam_dev)
        re = [recv[u, k].astype(jnp.float32) for k in range(half)]
        im = [recv[u, half + k].astype(jnp.float32) for k in range(half)]
        for t in range(half + 1):
            by_re = by_im = None
            for k in range(half):
                weight = 1.0 if 2 * (k + 1) == spec_total else 2.0
                term_re = re[k] * float(table[0, k, t] * weight)
                term_im = im[k] * float(table[1, k, t] * weight)
                by_re = term_re if by_re is None else by_re + term_re
                by_im = term_im if by_im is None else by_im + term_im
            result[t, rows, :] = by_re + by_im
            if 0 < t < half:
                result[spec_total - t, rows, :] = by_re - by_im
        return 0

    lax.fori_loop(0, tm_size, to_time, 0)

    def turn(t, _):
        out[t] = result[t].T
        return 0

    lax.fori_loop(0, spec_total, turn, 0)


def dedisperse(series, delays):
    tm_size, feed_size, spec_dev, beam_dev, chan_dev = series.shape
    spec_total = spec_dev * tm_size
    half = spec_total // 2
    chans, trials = delays.shape
    trial_dev = trials // tm_size
    beams = beam_dev * tm_size
    blocks = (tm_size, 2 * half, beam_dev, trial_dev)
    vmem = pl.BlockSpec(memory_space=pltpu.VMEM)
    return pl.pallas_call(
        dedisperse_kernel,
        out_shape=jax.ShapeDtypeStruct((spec_total, trial_dev, beams), jnp.float32),
        in_specs=[vmem] * 2,
        out_specs=vmem,
        scratch_shapes=[
            pltpu.VMEM((half, 2 * beam_dev, chans), jnp.bfloat16),
            pltpu.VMEM((half, chans, 2 * trials), jnp.bfloat16),
            pltpu.VMEM(blocks, jnp.bfloat16),
            pltpu.VMEM(blocks, jnp.bfloat16),
            pltpu.VMEM((spec_total, beams, trial_dev), jnp.float32),
            pltpu.SemaphoreType.DMA((tm_size,)),
            pltpu.SemaphoreType.DMA((tm_size,)),
        ],
        compiler_params=pltpu.CompilerParams(
            collective_id=1, has_side_effects=True, vmem_limit_bytes=48 * 1024 * 1024
        ),
        name="dedisperse",
    )(series, delays)


def local(voltages, feed_at_grid_slot, ew_grid, ns_grid, delays):
    tm_size = lax.axis_size("tm")
    feed_size = lax.axis_size("feed")
    slots = feed_at_grid_slot.reshape(ROWS, 8).T
    ew_row = (ew_grid[:, None] * jnp.arange(4, dtype=jnp.int32)[None, :]).reshape(1, -1)
    ns_row = ns_grid.reshape(1, -1)
    beam_dev = ew_grid.shape[0] * ns_grid.shape[0] // (tm_size * feed_size)
    series = search(voltages, slots, ew_row, ns_row, tm_size, feed_size, beam_dev)
    return dedisperse(series, delays).transpose(1, 2, 0)


def solution(mesh):
    in_specs = (P("feed", "tm"), P(), P(), P(), P())
    out_specs = P("tm", "feed", None)
    aligned = CHANS // mesh.shape["feed"] % 128 == 0
    body = local if aligned else local_unaligned
    return jax.shard_map(body, mesh=mesh, in_specs=in_specs, out_specs=out_specs, check_vma=False)
```

```python
from functools import partial
import math

import jax
import jax.numpy as jnp
import numpy as np
from jax import lax
from jax.experimental import pallas as pl
from jax.experimental.pallas import tpu as pltpu
from jax.sharding import PartitionSpec as P

NFFT = 2048
CHANS = 1024
TAPS = 4
ROWS = 256


TWO_PI = 2.0 * math.pi
phase_modulus = 1048576


def from_behind(block, axis, distance):
    devices = range(lax.axis_size(axis))
    route = [(i - distance, i) for i in devices if i - distance in devices]
    return lax.ppermute(block, axis, route)


def pfb_window(tap_count, series_length):
    points = jnp.arange(tap_count * series_length, dtype=jnp.float32) + 0.5
    start_offset = points / series_length - tap_count / 2.0
    taper = 0.5 - 0.5 * jnp.cos(TWO_PI * points / (tap_count * series_length))
    values = (jnp.sinc(start_offset) * taper).reshape(tap_count, series_length)
    return values / jnp.sqrt(jnp.sum(values * values, axis=0, keepdims=True))


def dft_table(series_length, columns):
    product = (
        jnp.arange(series_length, dtype=jnp.int32)[:, None]
        * jnp.arange(columns, dtype=jnp.int32)[None, :]
        % series_length
    )
    angles = product.astype(jnp.float32) * (TWO_PI / series_length)
    factor = 1.0 / math.sqrt(series_length)
    return jnp.concatenate([jnp.cos(angles) * factor, -jnp.sin(angles) * factor], axis=1).astype(
        jnp.bfloat16
    )


def spectral_table(series_length):
    product = (
        jnp.arange(series_length, dtype=jnp.int32)[:, None]
        * jnp.arange(series_length, dtype=jnp.int32)[None, :]
        % series_length
    )
    angles = product.astype(jnp.float32) * (TWO_PI / series_length)
    factor = 1.0 / math.sqrt(series_length)
    nonzero = (jnp.arange(series_length) > 0)[:, None]
    cosine = jnp.where(nonzero, jnp.cos(angles) * factor, 0.0)
    sine_part = jnp.where(nonzero, -jnp.sin(angles) * factor, 0.0)
    return jnp.stack([cosine, sine_part]).astype(jnp.bfloat16)


def steer_table(coords, grid_ids, chan_ids, factor):
    phases = (
        coords[None, None, :] * grid_ids[None, :, None] * chan_ids[:, None, None] % phase_modulus
    )
    angles = phases.astype(jnp.float32) * (TWO_PI / phase_modulus)
    return (
        (jnp.cos(angles) * factor).astype(jnp.bfloat16),
        (jnp.sin(angles) * factor).astype(jnp.bfloat16),
    )


def form_beams(block_in, feed_at_grid_slot, ew_tables, ns_tables):
    ew_real, ew_imag = ew_tables
    ns_real, ns_imag = ns_tables
    item_count = block_in.shape[1]
    chan_count = block_in.shape[3]
    gridded = jnp.take(block_in, feed_at_grid_slot, axis=0).reshape(
        ROWS, 4, 2, item_count, 2, chan_count
    )
    grid_real = gridded[:, :, :, :, 0, :]
    grid_imag = gridded[:, :, :, :, 1, :]
    east_mix = partial(jnp.einsum, "cey,rypsc->erpsc", preferred_element_type=jnp.float32)
    east_real = (east_mix(ew_real, grid_real) - east_mix(ew_imag, grid_imag)).astype(jnp.bfloat16)
    east_imag = (east_mix(ew_real, grid_imag) + east_mix(ew_imag, grid_real)).astype(jnp.bfloat16)
    north_mix = partial(jnp.einsum, "cbr,erpsc->ebpsc", preferred_element_type=jnp.float32)
    beam_real = north_mix(ns_real, east_real) - north_mix(ns_imag, east_imag)
    beam_imag = north_mix(ns_real, east_imag) + north_mix(ns_imag, east_real)
    beam_power = jnp.sum(beam_real * beam_real + beam_imag * beam_imag, axis=2)
    return beam_power.reshape(-1, item_count, chan_count).astype(jnp.bfloat16)


def local_unaligned(voltages, feed_at_grid_slot, ew_grid, ns_grid, delays):
    feed_dev = voltages.shape[0]
    spec_dev = voltages.shape[1] // NFFT
    time_extent = lax.axis_size("tm")
    feed_size = lax.axis_size("feed")
    spec_total = spec_dev * time_extent
    frames = (
        (voltages.astype(jnp.float32) / 64.0).astype(jnp.bfloat16).reshape(feed_dev, spec_dev, NFFT)
    )
    history = from_behind(frames[:, spec_dev - TAPS + 1 :, :], "tm", 1)
    padded = jnp.concatenate([history, frames], axis=1)
    window = pfb_window(TAPS, NFFT)
    filtered = jnp.zeros((feed_dev, spec_dev, NFFT), jnp.float32)
    for tap_index in range(TAPS):
        filtered = filtered + window[tap_index] * padded[
            :, tap_index : tap_index + spec_dev, :
        ].astype(jnp.float32)
    spectra = jnp.dot(
        filtered.astype(jnp.bfloat16).reshape(feed_dev * spec_dev, NFFT),
        dft_table(NFFT, CHANS),
        preferred_element_type=jnp.float32,
    )
    spectra = spectra.astype(jnp.bfloat16).reshape(feed_dev, spec_dev, 2, CHANS)
    chan_dev = CHANS // feed_size
    chan_ids = lax.axis_index("feed") * chan_dev + jnp.arange(chan_dev, dtype=jnp.int32) + CHANS
    ew_tables = steer_table(jnp.arange(4, dtype=jnp.int32), ew_grid, chan_ids, 0.5)
    ns_tables = steer_table(
        jnp.arange(ROWS, dtype=jnp.int32), ns_grid, chan_ids, 1.0 / math.sqrt(ROWS)
    )
    intensity = form_beams(
        lax.all_to_all(spectra, "feed", split_axis=3, concat_axis=0, tiled=True),
        feed_at_grid_slot,
        ew_tables,
        ns_tables,
    )
    time_table = spectral_table(spec_total)
    first_freq = lax.axis_index("tm") * spec_dev
    by_beam = lax.all_to_all(intensity, "feed", split_axis=0, concat_axis=2, tiled=True)
    my_table = lax.dynamic_slice_in_dim(time_table, first_freq, spec_dev, 1)
    zero_init = jnp.zeros((by_beam.shape[0], 2, spec_dev, CHANS), jnp.float32)
    spectrum = (
        zero_init
        + jnp.einsum(
            "rkt,btc->brkc",
            my_table,
            lax.all_gather(by_beam, "tm", axis=1, tiled=True),
            preferred_element_type=jnp.float32,
        )
    ).astype(jnp.bfloat16)
    freq_ids = first_freq + jnp.arange(spec_dev, dtype=jnp.int32)
    phases = freq_ids[:, None, None] * delays[None, :, :] % spec_total
    angles = phases.astype(jnp.float32) * (TWO_PI / spec_total)
    phase_real = jnp.cos(angles).astype(jnp.bfloat16)
    phase_imag = jnp.sin(angles).astype(jnp.bfloat16)
    shift_mixture = partial(jnp.einsum, "vuw,uwt->vut", preferred_element_type=jnp.float32)
    spec_real = spectrum[:, 0]
    spec_imag = spectrum[:, 1]
    moved_real = shift_mixture(spec_real, phase_real) - shift_mixture(spec_imag, phase_imag)
    moved_imag = shift_mixture(spec_real, phase_imag) + shift_mixture(spec_imag, phase_real)
    folded = (jnp.stack([moved_real, moved_imag], axis=1) * (1.0 / math.sqrt(CHANS))).astype(
        jnp.bfloat16
    )
    combined = lax.all_to_all(folded, "tm", split_axis=3, concat_axis=2, tiled=True)
    return jnp.einsum("brkd,rkt->dbt", combined, time_table, preferred_element_type=jnp.float32)


MESH = pl.DeviceIdType.MESH
REACH = 8


def sincos(phases, modulus):
    quarter = modulus // 4
    quadrant = (phases + quarter // 2) >> (quarter.bit_length() - 1)
    rest = (phases - quadrant * quarter).astype(jnp.float32) * (TWO_PI / modulus)
    square = rest * rest
    sine = rest * (
        1.0 + square * (-1.0 / 6 + square * (1.0 / 120 + square * (-1.0 / 5040 + square / 362880)))
    )
    cosine = 1.0 + square * (
        -0.5 + square * (1.0 / 24 + square * (-1.0 / 720 + square * (1.0 / 40320)))
    )
    swap = quadrant & 1 == 1
    first = jnp.where(swap, sine, cosine)
    second = jnp.where(swap, cosine, sine)
    turned = quadrant & 3
    return (
        jnp.where((turned == 1) | (turned == 2), -first, first),
        jnp.where(turned >= 2, -second, second),
    )


def window_constant(tap_count, series_length):
    points = np.arange(tap_count * series_length, dtype=np.float64) + 0.5
    offset = points / series_length - tap_count / 2.0
    taper = 0.5 - 0.5 * np.cos(TWO_PI * points / (tap_count * series_length))
    values = (np.sinc(offset) * taper).reshape(tap_count, series_length)
    values = values / np.sqrt(np.sum(values * values, axis=0, keepdims=True))
    return (values / 64.0).astype(np.float32)


def dft_constant(series_length, columns, blocks):
    product = np.outer(np.arange(columns), np.arange(series_length)) % series_length
    angles = product * (TWO_PI / series_length)
    factor = 1.0 / math.sqrt(series_length)
    table = np.stack([np.cos(angles) * factor, -np.sin(angles) * factor])
    table = table.reshape(2, blocks, columns // blocks, series_length).transpose(1, 0, 2, 3)
    return table.reshape(blocks, -1, series_length).astype(jnp.bfloat16)


def search_kernel(
    volt, window, twiddle_hbm, slots, ew_row, ns_row, out,
    raw, frames, hist, filtered, send, spec, twiddle, placed_v, grid, east, steer, coarse, fine,
    power, beams, raw_s, twiddle_s, hist_ss, hist_rs, spec_ss, spec_rs, beam_ss, beam_rs,
):
    spec_dev, feed_dev, length = frames.shape
    feed_size = spec.shape[1]
    chan_dev = spec.shape[2] // 2
    tm_size = out.shape[0]
    beam_dev, ns_beams = out.shape[3], power.shape[3]
    pairs = power.shape[2]
    ews = pairs // 2
    tm = lax.axis_index("tm")
    feed = lax.axis_index("feed")
    after = lax.rem(tm + 1, tm_size)

    def other_device(step):
        other = lax.rem(tm * feed_size + feed + step, tm_size * feed_size)
        return other // feed_size, lax.rem(other, feed_size)

    barrier = pltpu.get_barrier_semaphore()

    def greet(step, _):
        pl.semaphore_signal(barrier, inc=1, device_id=other_device(step), device_id_type=MESH)
        return 0

    lax.fori_loop(1, tm_size * feed_size, greet, 0)

    def raw_copy(s):
        return pltpu.make_async_copy(
            volt.at[:, pl.ds(s * length, length)], raw.at[s % 2], raw_s.at[s % 2]
        )

    twiddle_copy = pltpu.make_async_copy(twiddle_hbm, twiddle, twiddle_s)
    raw_copy(spec_dev - 1).start()
    raw_copy(spec_dev - 2).start()
    twiddle_copy.start()

    step_rows = 16

    def convert(s):
        def body(i, _):
            rows = pl.ds(pl.multiple_of(i * step_rows, step_rows), step_rows)
            frames[s, rows, :] = raw[s % 2, rows, :].astype(jnp.float32).astype(jnp.bfloat16)
            return 0

        raw_copy(s).wait()
        lax.fori_loop(0, feed_dev // step_rows, body, 0)
        if s >= 2:
            raw_copy(s - 2).start()

    def history(i):
        return pltpu.make_async_remote_copy(
            src_ref=frames.at[spec_dev - TAPS + 1 + i],
            dst_ref=hist.at[i],
            send_sem=hist_ss.at[i],
            recv_sem=hist_rs.at[i],
            device_id=(after, feed),
            device_id_type=MESH,
        )

    convert(spec_dev - 1)
    pl.semaphore_wait(barrier, tm_size * feed_size - 1)
    history(TAPS - 2).start()
    for s in range(spec_dev - 2, -1, -1):
        convert(s)
    twiddle_copy.wait()

    live = jnp.where(tm > 0, 1.0, 0.0).astype(jnp.float32)

    def spec_copy(s, other, slot):
        return pltpu.make_async_remote_copy(
            src_ref=send.at[s, other],
            dst_ref=spec.at[s, slot],
            send_sem=spec_ss.at[s, other],
            recv_sem=spec_rs.at[s, slot],
            device_id=(tm, other),
            device_id_type=MESH,
        )

    def channelize(s):
        if s < TAPS - 1:
            history(s).wait_recv()

        def filter_rows(i, _):
            rows = pl.ds(pl.multiple_of(i * step_rows, step_rows), step_rows)
            total = None
            for tap in range(TAPS):
                at = s + tap - (TAPS - 1)
                weights = window[tap : tap + 1, :]
                if at < 0:
                    term = hist[TAPS - 1 + at, rows, :].astype(jnp.float32) * (weights * live)
                else:
                    term = frames[at, rows, :].astype(jnp.float32) * weights
                total = term if total is None else total + term
            filtered[rows, :] = total.astype(jnp.bfloat16)
            return 0

        lax.fori_loop(0, feed_dev // step_rows, filter_rows, 0)

        def transform(i, _):
            other = lax.rem(feed + 1 + i, feed_size)
            block = lax.dot_general(
                twiddle[other],
                filtered[...],
                (((1,), (1,)), ((), ())),
                preferred_element_type=jnp.float32,
            ).astype(jnp.bfloat16)

            @pl.when(other != feed)
            def _():
                send[s, other] = block
                spec_copy(s, other, feed).start()

            @pl.when(other == feed)
            def _():
                spec[s, other] = block

            return 0

        lax.fori_loop(0, feed_size, transform, 0)

    def make_tables():
        def one_hot(i, _):
            rows = pl.ds(pl.multiple_of(i * step_rows, step_rows), step_rows)
            shape = (step_rows, placed_v.shape[2])
            feeds = lax.broadcasted_iota(jnp.int32, shape, 0) + i * step_rows
            for m in range(placed_v.shape[0]):
                hit = feeds == slots[m : m + 1, :]
                placed_v[m, rows, :] = jnp.where(hit, 1.0, 0.0).astype(jnp.bfloat16)
            return 0

        lax.fori_loop(0, placed_v.shape[1] // step_rows, one_hot, 0)
        first = feed * chan_dev + CHANS
        chans = lax.broadcasted_iota(jnp.int32, (chan_dev, 4 * ews), 0) + first
        turns = sincos((ew_row[...] * chans) & (phase_modulus - 1), phase_modulus)
        for part, value in enumerate(turns):
            value = (value * 0.5).astype(jnp.bfloat16).astype(jnp.float32)
            steer[:, part * 4 * ews : (part + 1) * 4 * ews] = value
        centres, reach = coarse.shape[2], fine.shape[2]
        centre_ids = lax.broadcasted_iota(jnp.int32, (centres, ns_beams), 0) * (4 * reach)
        centre_ids = centre_ids + (2 * reach - 1)
        reach_ids = lax.broadcasted_iota(jnp.int32, (reach, ns_beams), 0) * 2 + 1
        half_modulus = 2 * phase_modulus
        factor = 1.0 / math.sqrt(ROWS)

        def rotations(c, _):
            step = (ns_row[...] * (first + c)) & (phase_modulus - 1)
            for ids, table, size in ((centre_ids, coarse, factor), (reach_ids, fine, 1.0)):
                re, im = sincos((ids * step) & (half_modulus - 1), half_modulus)
                table[0, c] = re * size
                table[1, c] = im * size
            return 0

        lax.fori_loop(0, chan_dev, rotations, 0)

    def arrive(s):
        def body(step, _):
            other = lax.rem(feed + step, feed_size)
            spec_copy(s, other, other).wait()
            return 0

        lax.fori_loop(1, feed_size, body, 0)

    def place(s):
        def body(m, _):
            total = jnp.zeros(grid.shape[1:], jnp.float32)
            for j in range(feed_size):
                total += jnp.dot(
                    spec[s, j],
                    placed_v[m, j * feed_dev : (j + 1) * feed_dev, :],
                    preferred_element_type=jnp.float32,
                )
            grid[m] = total
            return 0

        lax.fori_loop(0, grid.shape[0], body, 0)

    def mix_east(at):
        def body(i, _):
            start = pl.multiple_of(i * 8, 8)
            rows = pl.ds(start, 8)
            rows_im = pl.ds(pl.multiple_of(chan_dev + start, 8), 8)
            for pol in range(2):
                re = [grid[2 * y + pol, rows, :] for y in range(4)]
                im = [grid[2 * y + pol, rows_im, :] for y in range(4)]
                for e in range(ews):
                    sum_re = sum_im = None
                    for y in range(4):
                        w = e * 4 + y
                        w_re = steer[rows, w : w + 1]
                        w_im = steer[rows, 4 * ews + w : 4 * ews + w + 1]
                        term_re = w_re * re[y] - w_im * im[y]
                        term_im = w_re * im[y] + w_im * re[y]
                        sum_re = term_re if sum_re is None else sum_re + term_re
                        sum_im = term_im if sum_im is None else sum_im + term_im
                    row = at * 2 * pairs + pol * ews + e
                    east[rows, row, :] = sum_re
                    east[rows, row + pairs, :] = sum_im
            return 0

        lax.fori_loop(0, chan_dev // 8, body, 0)

    def mix_north(count):
        def channel(c):
            fine_re, fine_im = fine[0, c], fine[1, c]
            parts_re, parts_im = [], []
            for r in range(coarse.shape[2]):
                a_re, a_im = coarse[0, c, r : r + 1, :], coarse[1, c, r : r + 1, :]
                rr, ii, ri, ir = a_re * fine_re, a_im * fine_im, a_re * fine_im, a_im * fine_re
                parts_re.append(jnp.concatenate([rr - ii, rr + ii], axis=0).astype(jnp.bfloat16))
                parts_im.append(jnp.concatenate([ir + ri, ir - ri], axis=0).astype(jnp.bfloat16))
            side = east[c, : count * 2 * pairs, :].astype(jnp.bfloat16)
            by_re = jnp.dot(
                side, jnp.concatenate(parts_re, axis=0), preferred_element_type=jnp.float32
            )
            by_im = jnp.dot(
                side, jnp.concatenate(parts_im, axis=0), preferred_element_type=jnp.float32
            )
            for k in range(count):
                lo, mid, hi = 2 * k * pairs, (2 * k + 1) * pairs, (2 * k + 2) * pairs
                beam_re = by_re[lo:mid] - by_im[mid:hi]
                beam_im = by_re[mid:hi] + by_im[lo:mid]
                power[k, c] = beam_re * beam_re + beam_im * beam_im

        def body(i, _):
            for c in range(4):
                channel(i * 4 + c)
            return 0

        lax.fori_loop(0, chan_dev // 4, body, 0)

    def transpose_power(s, k):
        width = beam_dev * tm_size
        for e in range(ews):
            total = power[k, :, e, :] + power[k, :, ews + e, :]
            turned = total.T.astype(jnp.bfloat16)
            for part in range(ns_beams // beam_dev):
                first = e * ns_beams + part * beam_dev
                block = turned[part * beam_dev : (part + 1) * beam_dev]
                beams[first % width // beam_dev, first // width, s] = block

    def beam_copy(first, last, group, peer, slot):
        return pltpu.make_async_remote_copy(
            src_ref=beams.at[peer[0], peer[1], pl.ds(first, last - first)],
            dst_ref=out.at[slot[0], slot[1], pl.ds(first, last - first)],
            send_sem=beam_ss.at[group, peer[0], peer[1]],
            recv_sem=beam_rs.at[group, slot[0], slot[1]],
            device_id=peer,
            device_id_type=MESH,
        )

    middle = spec_dev // 2
    groups = [(spec_dev - 1, middle), (middle - 1, 0)]

    def form(group):
        high, low = groups[group]
        mix_north(high + 1 - low)
        for k, s in enumerate(range(low, high + 1)):
            transpose_power(s, k)

        def go(step, _):
            beam_copy(low, high + 1, group, other_device(step), (tm, feed)).start()
            return 0

        lax.fori_loop(1, tm_size * feed_size, go, 0)
        out[tm, feed, low : high + 1] = beams[tm, feed, low : high + 1]

    def gather_east(s):
        arrive(s)
        place(s)
        mix_east(s - middle if s >= middle else s)

    channelize(spec_dev - 1)
    make_tables()
    waiting = TAPS - 3
    for s in range(spec_dev - 2, -1, -1):
        if waiting >= 0:
            history(waiting + 1).wait_send()
            history(waiting).start()
            waiting -= 1
        channelize(s)
        if s + 1 > middle:
            gather_east(s + 1)
        if s == middle - 1:
            gather_east(middle)
    form(0)
    for s in range(middle - 1, -1, -1):
        gather_east(s)
    form(1)
    for group, (high, low) in enumerate(groups):
        def finish(step, _):
            peer = other_device(step)
            beam_copy(low, high + 1, group, peer, peer).wait()
            return 0

        lax.fori_loop(1, tm_size * feed_size, finish, 0)
    history(0).wait_send()


def search(voltages, slots, ew_row, ns_row, tm_size, feed_size, beam_dev):
    feed_dev = voltages.shape[0]
    spec_dev = voltages.shape[1] // NFFT
    chan_dev = CHANS // feed_size
    ns_beams = ns_row.shape[1]
    pairs = 2 * ew_row.shape[1] // 4
    window = jnp.asarray(window_constant(TAPS, NFFT))
    twiddle = jnp.asarray(dft_constant(NFFT, CHANS, feed_size))
    blocks = (spec_dev, feed_size, 2 * chan_dev, feed_dev)
    batch = spec_dev - spec_dev // 2
    vmem = pl.BlockSpec(memory_space=pltpu.VMEM)
    hbm = pl.BlockSpec(memory_space=pl.ANY)
    dma = pltpu.SemaphoreType.DMA
    sent = (tm_size, feed_size, spec_dev, beam_dev, chan_dev)
    return pl.pallas_call(
        search_kernel,
        out_shape=jax.ShapeDtypeStruct(sent, jnp.bfloat16),
        in_specs=[hbm, vmem, hbm, vmem, vmem, vmem],
        out_specs=vmem,
        scratch_shapes=[
            pltpu.VMEM((2, feed_dev, NFFT), jnp.int32),
            pltpu.VMEM((spec_dev, feed_dev, NFFT), jnp.bfloat16),
            pltpu.VMEM((TAPS - 1, feed_dev, NFFT), jnp.bfloat16),
            pltpu.VMEM((feed_dev, NFFT), jnp.bfloat16),
            pltpu.VMEM(blocks, jnp.bfloat16),
            pltpu.VMEM(blocks, jnp.bfloat16),
            pltpu.VMEM(twiddle.shape, jnp.bfloat16),
            pltpu.VMEM((slots.shape[0], slots.size, ROWS), jnp.bfloat16),
            pltpu.VMEM((slots.shape[0], 2 * chan_dev, ROWS), jnp.float32),
            pltpu.VMEM((chan_dev, batch * 2 * pairs, ROWS), jnp.float32),
            pltpu.VMEM((chan_dev, 2 * ew_row.shape[1]), jnp.float32),
            pltpu.VMEM((2, chan_dev, ROWS // (2 * REACH), ns_beams), jnp.float32),
            pltpu.VMEM((2, chan_dev, REACH, ns_beams), jnp.float32),
            pltpu.VMEM((batch, chan_dev, pairs, ns_beams), jnp.float32),
            pltpu.VMEM(sent, jnp.bfloat16),
            dma((2,)),
            dma(()),
            dma((TAPS - 1,)),
            dma((TAPS - 1,)),
            dma((spec_dev, feed_size)),
            dma((spec_dev, feed_size)),
            dma((2, tm_size, feed_size)),
            dma((2, tm_size, feed_size)),
        ],
        compiler_params=pltpu.CompilerParams(
            collective_id=0, has_side_effects=True, vmem_limit_bytes=60 * 1024 * 1024
        ),
        name="search",
    )(voltages, window, twiddle, slots, ew_row, ns_row)


def transform_table(spec_total):
    ids = np.outer(np.arange(1, spec_total // 2 + 1), np.arange(spec_total)) % spec_total
    turn = ids * (TWO_PI / spec_total)
    table = np.stack([np.cos(turn), -np.sin(turn)]) / math.sqrt(spec_total)
    return table.astype(jnp.bfloat16).astype(np.float64)


def dedisperse_kernel(series, delays, out, freq, phase, send, recv, result, send_s, recv_s):
    tm_size, feed_size, spec_dev, beam_dev, chan_dev = series.shape
    spec_total = spec_dev * tm_size
    half = spec_total // 2
    trials = delays.shape[1]
    trial_dev = trials // tm_size
    table = transform_table(spec_total)
    tm = lax.axis_index("tm")
    feed = lax.axis_index("feed")

    barrier = pltpu.get_barrier_semaphore()
    for step in range(1, tm_size):
        other = lax.rem(tm + step, tm_size)
        pl.semaphore_signal(barrier, inc=1, device_id=(other, feed), device_id_type=MESH)

    def to_frequency(f, _):
        lanes = pl.ds(pl.multiple_of(f * chan_dev, chan_dev), chan_dev)
        x = [
            series[t // spec_dev, f, t % spec_dev].astype(jnp.float32) for t in range(spec_total)
        ]
        even = [x[t] + x[spec_total - t] for t in range(1, half)]
        odd = [x[t] - x[spec_total - t] for t in range(1, half)]
        for k in range(half):
            re = x[0] * float(table[0, k, 0]) + x[half] * float(table[0, k, half])
            im = None
            for t in range(1, half):
                re = re + even[t - 1] * float(table[0, k, t])
                term = odd[t - 1] * float(table[1, k, t])
                im = term if im is None else im + term
            freq[k, :beam_dev, lanes] = re.astype(jnp.bfloat16)
            freq[k, beam_dev:, lanes] = im.astype(jnp.bfloat16)
        return 0

    lax.fori_loop(0, feed_size, to_frequency, 0)

    step_rows = 16

    def make_phase(i, _):
        rows = pl.ds(pl.multiple_of(i * step_rows, step_rows), step_rows)
        base_re, base_im = sincos(delays[rows, :] & (spec_total - 1), spec_total)
        re, im = base_re, base_im
        for k in range(half):
            phase[k, rows, :trials] = re.astype(jnp.bfloat16)
            phase[k, rows, trials:] = im.astype(jnp.bfloat16)
            re, im = re * base_re - im * base_im, re * base_im + im * base_re
        return 0

    lax.fori_loop(0, delays.shape[0] // step_rows, make_phase, 0)

    def move(k, _):
        mixed = jnp.dot(freq[k], phase[k], preferred_element_type=jnp.float32)
        factor = 1.0 / math.sqrt(CHANS)
        re = (mixed[:beam_dev, :trials] - mixed[beam_dev:, trials:]) * factor
        im = (mixed[:beam_dev, trials:] + mixed[beam_dev:, :trials]) * factor
        for u in range(tm_size):
            part = slice(u * trial_dev, (u + 1) * trial_dev)
            send[u, 2 * k] = re[:, part].astype(jnp.bfloat16)
            send[u, 2 * k + 1] = im[:, part].astype(jnp.bfloat16)
        return 0

    def exchange(part, other, slot):
        ids = pl.ds(part * half, half)
        return pltpu.make_async_remote_copy(
            src_ref=send.at[other, ids],
            dst_ref=recv.at[slot, ids],
            send_sem=send_s.at[part, other],
            recv_sem=recv_s.at[part, slot],
            device_id=(other, feed),
            device_id_type=MESH,
        )

    edges = (0, half // 2, half)
    pl.semaphore_wait(barrier, tm_size - 1)
    for part in range(2):
        lax.fori_loop(edges[part], edges[part + 1], move, 0)
        for step in range(1, tm_size):
            exchange(part, lax.rem(tm + step, tm_size), tm).start()
    recv[tm] = send[tm]
    for part in range(2):
        for step in range(1, tm_size):
            other = lax.rem(tm + step, tm_size)
            exchange(part, other, other).wait()

    def to_time(u, _):
        rows = pl.ds(pl.multiple_of(u * beam_dev, beam_dev), beam_dev)
        re = [recv[u, 2 * k].astype(jnp.float32) for k in range(half)]
        im = [recv[u, 2 * k + 1].astype(jnp.float32) for k in range(half)]
        for t in range(half + 1):
            by_re = by_im = None
            for k in range(half):
                weight = 1.0 if 2 * (k + 1) == spec_total else 2.0
                term_re = re[k] * float(table[0, k, t] * weight)
                term_im = im[k] * float(table[1, k, t] * weight)
                by_re = term_re if by_re is None else by_re + term_re
                by_im = term_im if by_im is None else by_im + term_im
            result[t, rows, :] = by_re + by_im
            if 0 < t < half:
                result[spec_total - t, rows, :] = by_re - by_im
        return 0

    lax.fori_loop(0, tm_size, to_time, 0)

    def turn(t, _):
        out[t] = result[t].T
        return 0

    lax.fori_loop(0, spec_total, turn, 0)


def dedisperse(series, delays):
    tm_size, feed_size, spec_dev, beam_dev, chan_dev = series.shape
    spec_total = spec_dev * tm_size
    half = spec_total // 2
    chans, trials = delays.shape
    trial_dev = trials // tm_size
    beams = beam_dev * tm_size
    blocks = (tm_size, 2 * half, beam_dev, trial_dev)
    vmem = pl.BlockSpec(memory_space=pltpu.VMEM)
    return pl.pallas_call(
        dedisperse_kernel,
        out_shape=jax.ShapeDtypeStruct((spec_total, trial_dev, beams), jnp.float32),
        in_specs=[vmem] * 2,
        out_specs=vmem,
        scratch_shapes=[
            pltpu.VMEM((half, 2 * beam_dev, chans), jnp.bfloat16),
            pltpu.VMEM((half, chans, 2 * trials), jnp.bfloat16),
            pltpu.VMEM(blocks, jnp.bfloat16),
            pltpu.VMEM(blocks, jnp.bfloat16),
            pltpu.VMEM((spec_total, beams, trial_dev), jnp.float32),
            pltpu.SemaphoreType.DMA((2, tm_size)),
            pltpu.SemaphoreType.DMA((2, tm_size)),
        ],
        compiler_params=pltpu.CompilerParams(
            collective_id=1, has_side_effects=True, vmem_limit_bytes=48 * 1024 * 1024
        ),
        name="dedisperse",
    )(series, delays)


def local(voltages, feed_at_grid_slot, ew_grid, ns_grid, delays):
    tm_size = lax.axis_size("tm")
    feed_size = lax.axis_size("feed")
    slots = feed_at_grid_slot.reshape(-1, 2, REACH, 8)
    slots = jnp.stack([slots[:, 1], slots[:, 0, ::-1]], axis=1).reshape(ROWS, 8).T
    ew_row = (ew_grid[:, None] * jnp.arange(4, dtype=jnp.int32)[None, :]).reshape(1, -1)
    ns_row = ns_grid.reshape(1, -1)
    beam_dev = ew_grid.shape[0] * ns_grid.shape[0] // (tm_size * feed_size)
    series = search(voltages, slots, ew_row, ns_row, tm_size, feed_size, beam_dev)
    return dedisperse(series, delays).transpose(1, 2, 0)


def solution(mesh):
    in_specs = (P("feed", "tm"), P(), P(), P(), P())
    out_specs = P("tm", "feed", None)
    aligned = CHANS // mesh.shape["feed"] % 128 == 0
    body = local if aligned else local_unaligned
    return jax.shard_map(body, mesh=mesh, in_specs=in_specs, out_specs=out_specs, check_vma=False)
```

```python
from functools import partial
import math

import jax
import jax.numpy as jnp
import numpy as np
from jax import lax
from jax.experimental import pallas as pl
from jax.experimental.pallas import tpu as pltpu
from jax.sharding import PartitionSpec as P

NFFT = 2048
CHANS = 1024
TAPS = 4
ROWS = 256


TWO_PI = 2.0 * math.pi
phase_modulus = 1048576


def from_behind(block, axis, distance):
    devices = range(lax.axis_size(axis))
    route = [(i - distance, i) for i in devices if i - distance in devices]
    return lax.ppermute(block, axis, route)


def pfb_window(tap_count, series_length):
    points = jnp.arange(tap_count * series_length, dtype=jnp.float32) + 0.5
    start_offset = points / series_length - tap_count / 2.0
    taper = 0.5 - 0.5 * jnp.cos(TWO_PI * points / (tap_count * series_length))
    values = (jnp.sinc(start_offset) * taper).reshape(tap_count, series_length)
    return values / jnp.sqrt(jnp.sum(values * values, axis=0, keepdims=True))


def dft_table(series_length, columns):
    product = (
        jnp.arange(series_length, dtype=jnp.int32)[:, None]
        * jnp.arange(columns, dtype=jnp.int32)[None, :]
        % series_length
    )
    angles = product.astype(jnp.float32) * (TWO_PI / series_length)
    factor = 1.0 / math.sqrt(series_length)
    return jnp.concatenate([jnp.cos(angles) * factor, -jnp.sin(angles) * factor], axis=1).astype(
        jnp.bfloat16
    )


def spectral_table(series_length):
    product = (
        jnp.arange(series_length, dtype=jnp.int32)[:, None]
        * jnp.arange(series_length, dtype=jnp.int32)[None, :]
        % series_length
    )
    angles = product.astype(jnp.float32) * (TWO_PI / series_length)
    factor = 1.0 / math.sqrt(series_length)
    nonzero = (jnp.arange(series_length) > 0)[:, None]
    cosine = jnp.where(nonzero, jnp.cos(angles) * factor, 0.0)
    sine_part = jnp.where(nonzero, -jnp.sin(angles) * factor, 0.0)
    return jnp.stack([cosine, sine_part]).astype(jnp.bfloat16)


def steer_table(coords, grid_ids, chan_ids, factor):
    phases = (
        coords[None, None, :] * grid_ids[None, :, None] * chan_ids[:, None, None] % phase_modulus
    )
    angles = phases.astype(jnp.float32) * (TWO_PI / phase_modulus)
    return (
        (jnp.cos(angles) * factor).astype(jnp.bfloat16),
        (jnp.sin(angles) * factor).astype(jnp.bfloat16),
    )


def form_beams(block_in, feed_at_grid_slot, ew_tables, ns_tables):
    ew_real, ew_imag = ew_tables
    ns_real, ns_imag = ns_tables
    item_count = block_in.shape[1]
    chan_count = block_in.shape[3]
    gridded = jnp.take(block_in, feed_at_grid_slot, axis=0).reshape(
        ROWS, 4, 2, item_count, 2, chan_count
    )
    grid_real = gridded[:, :, :, :, 0, :]
    grid_imag = gridded[:, :, :, :, 1, :]
    east_mix = partial(jnp.einsum, "cey,rypsc->erpsc", preferred_element_type=jnp.float32)
    east_real = (east_mix(ew_real, grid_real) - east_mix(ew_imag, grid_imag)).astype(jnp.bfloat16)
    east_imag = (east_mix(ew_real, grid_imag) + east_mix(ew_imag, grid_real)).astype(jnp.bfloat16)
    north_mix = partial(jnp.einsum, "cbr,erpsc->ebpsc", preferred_element_type=jnp.float32)
    beam_real = north_mix(ns_real, east_real) - north_mix(ns_imag, east_imag)
    beam_imag = north_mix(ns_real, east_imag) + north_mix(ns_imag, east_real)
    beam_power = jnp.sum(beam_real * beam_real + beam_imag * beam_imag, axis=2)
    return beam_power.reshape(-1, item_count, chan_count).astype(jnp.bfloat16)


def local_unaligned(voltages, feed_at_grid_slot, ew_grid, ns_grid, delays):
    feed_dev = voltages.shape[0]
    spec_dev = voltages.shape[1] // NFFT
    time_extent = lax.axis_size("tm")
    feed_size = lax.axis_size("feed")
    spec_total = spec_dev * time_extent
    frames = (
        (voltages.astype(jnp.float32) / 64.0).astype(jnp.bfloat16).reshape(feed_dev, spec_dev, NFFT)
    )
    history = from_behind(frames[:, spec_dev - TAPS + 1 :, :], "tm", 1)
    padded = jnp.concatenate([history, frames], axis=1)
    window = pfb_window(TAPS, NFFT)
    filtered = jnp.zeros((feed_dev, spec_dev, NFFT), jnp.float32)
    for tap_index in range(TAPS):
        filtered = filtered + window[tap_index] * padded[
            :, tap_index : tap_index + spec_dev, :
        ].astype(jnp.float32)
    spectra = jnp.dot(
        filtered.astype(jnp.bfloat16).reshape(feed_dev * spec_dev, NFFT),
        dft_table(NFFT, CHANS),
        preferred_element_type=jnp.float32,
    )
    spectra = spectra.astype(jnp.bfloat16).reshape(feed_dev, spec_dev, 2, CHANS)
    chan_dev = CHANS // feed_size
    chan_ids = lax.axis_index("feed") * chan_dev + jnp.arange(chan_dev, dtype=jnp.int32) + CHANS
    ew_tables = steer_table(jnp.arange(4, dtype=jnp.int32), ew_grid, chan_ids, 0.5)
    ns_tables = steer_table(
        jnp.arange(ROWS, dtype=jnp.int32), ns_grid, chan_ids, 1.0 / math.sqrt(ROWS)
    )
    intensity = form_beams(
        lax.all_to_all(spectra, "feed", split_axis=3, concat_axis=0, tiled=True),
        feed_at_grid_slot,
        ew_tables,
        ns_tables,
    )
    time_table = spectral_table(spec_total)
    first_freq = lax.axis_index("tm") * spec_dev
    by_beam = lax.all_to_all(intensity, "feed", split_axis=0, concat_axis=2, tiled=True)
    my_table = lax.dynamic_slice_in_dim(time_table, first_freq, spec_dev, 1)
    zero_init = jnp.zeros((by_beam.shape[0], 2, spec_dev, CHANS), jnp.float32)
    spectrum = (
        zero_init
        + jnp.einsum(
            "rkt,btc->brkc",
            my_table,
            lax.all_gather(by_beam, "tm", axis=1, tiled=True),
            preferred_element_type=jnp.float32,
        )
    ).astype(jnp.bfloat16)
    freq_ids = first_freq + jnp.arange(spec_dev, dtype=jnp.int32)
    phases = freq_ids[:, None, None] * delays[None, :, :] % spec_total
    angles = phases.astype(jnp.float32) * (TWO_PI / spec_total)
    phase_real = jnp.cos(angles).astype(jnp.bfloat16)
    phase_imag = jnp.sin(angles).astype(jnp.bfloat16)
    shift_mixture = partial(jnp.einsum, "vuw,uwt->vut", preferred_element_type=jnp.float32)
    spec_real = spectrum[:, 0]
    spec_imag = spectrum[:, 1]
    moved_real = shift_mixture(spec_real, phase_real) - shift_mixture(spec_imag, phase_imag)
    moved_imag = shift_mixture(spec_real, phase_imag) + shift_mixture(spec_imag, phase_real)
    folded = (jnp.stack([moved_real, moved_imag], axis=1) * (1.0 / math.sqrt(CHANS))).astype(
        jnp.bfloat16
    )
    combined = lax.all_to_all(folded, "tm", split_axis=3, concat_axis=2, tiled=True)
    return jnp.einsum("brkd,rkt->dbt", combined, time_table, preferred_element_type=jnp.float32)


MESH = pl.DeviceIdType.MESH
REACH = 8


def sincos(phases, modulus):
    quarter = modulus // 4
    quadrant = (phases + quarter // 2) >> (quarter.bit_length() - 1)
    rest = (phases - quadrant * quarter).astype(jnp.float32) * (TWO_PI / modulus)
    square = rest * rest
    sine = rest * (
        1.0 + square * (-1.0 / 6 + square * (1.0 / 120 + square * (-1.0 / 5040 + square / 362880)))
    )
    cosine = 1.0 + square * (
        -0.5 + square * (1.0 / 24 + square * (-1.0 / 720 + square * (1.0 / 40320)))
    )
    swap = quadrant & 1 == 1
    first = jnp.where(swap, sine, cosine)
    second = jnp.where(swap, cosine, sine)
    turned = quadrant & 3
    return (
        jnp.where((turned == 1) | (turned == 2), -first, first),
        jnp.where(turned >= 2, -second, second),
    )


def window_constant(tap_count, series_length):
    points = np.arange(tap_count * series_length, dtype=np.float64) + 0.5
    offset = points / series_length - tap_count / 2.0
    taper = 0.5 - 0.5 * np.cos(TWO_PI * points / (tap_count * series_length))
    values = (np.sinc(offset) * taper).reshape(tap_count, series_length)
    values = values / np.sqrt(np.sum(values * values, axis=0, keepdims=True))
    return (values / 64.0).astype(np.float32)


def dft_constant(series_length, columns, blocks):
    product = np.outer(np.arange(columns), np.arange(series_length)) % series_length
    angles = product * (TWO_PI / series_length)
    factor = 1.0 / math.sqrt(series_length)
    table = np.stack([np.cos(angles) * factor, -np.sin(angles) * factor])
    table = table.reshape(2, blocks, columns // blocks, series_length).transpose(1, 0, 2, 3)
    return table.reshape(blocks, -1, series_length).astype(jnp.bfloat16)


def search_kernel(
    volt, window, twiddle_hbm, slots, ew_row, ns_row, out,
    raw, frames, hist, filtered, send, spec, twiddle, placed_v, grid, east, steer, coarse, fine,
    power, beams, raw_s, twiddle_s, hist_ss, hist_rs, spec_ss, spec_rs, beam_ss, beam_rs,
):
    spec_dev, feed_dev, length = frames.shape
    feed_size = spec.shape[1]
    chan_dev = spec.shape[2] // 2
    tm_size = out.shape[0]
    beam_dev, ns_beams = out.shape[3], power.shape[3]
    pairs = power.shape[2]
    ews = pairs // 2
    tm = lax.axis_index("tm")
    feed = lax.axis_index("feed")
    after = lax.rem(tm + 1, tm_size)

    def other_device(step):
        other = lax.rem(tm * feed_size + feed + step, tm_size * feed_size)
        return other // feed_size, lax.rem(other, feed_size)

    barrier = pltpu.get_barrier_semaphore()

    def greet(step, _):
        pl.semaphore_signal(barrier, inc=1, device_id=other_device(step), device_id_type=MESH)
        return 0

    lax.fori_loop(1, tm_size * feed_size, greet, 0)

    def raw_copy(s):
        return pltpu.make_async_copy(
            volt.at[:, pl.ds(s * length, length)], raw.at[s % 2], raw_s.at[s % 2]
        )

    twiddle_copy = pltpu.make_async_copy(twiddle_hbm, twiddle, twiddle_s)
    raw_copy(spec_dev - 1).start()
    raw_copy(spec_dev - 2).start()
    twiddle_copy.start()

    step_rows = 16

    def convert(s):
        def body(i, _):
            rows = pl.ds(pl.multiple_of(i * step_rows, step_rows), step_rows)
            frames[s, rows, :] = raw[s % 2, rows, :].astype(jnp.float32).astype(jnp.bfloat16)
            return 0

        raw_copy(s).wait()
        lax.fori_loop(0, feed_dev // step_rows, body, 0)
        if s >= 2:
            raw_copy(s - 2).start()

    def history(i):
        return pltpu.make_async_remote_copy(
            src_ref=frames.at[spec_dev - TAPS + 1 + i],
            dst_ref=hist.at[i],
            send_sem=hist_ss.at[i],
            recv_sem=hist_rs.at[i],
            device_id=(after, feed),
            device_id_type=MESH,
        )

    convert(spec_dev - 1)
    pl.semaphore_wait(barrier, tm_size * feed_size - 1)
    history(TAPS - 2).start()
    for s in range(spec_dev - 2, -1, -1):
        convert(s)
    twiddle_copy.wait()

    live = jnp.where(tm > 0, 1.0, 0.0).astype(jnp.float32)

    def spec_copy(s, other, slot):
        return pltpu.make_async_remote_copy(
            src_ref=send.at[s, other],
            dst_ref=spec.at[s, slot],
            send_sem=spec_ss.at[s, other],
            recv_sem=spec_rs.at[s, slot],
            device_id=(tm, other),
            device_id_type=MESH,
        )

    def channelize(s):
        if s < TAPS - 1:
            history(s).wait_recv()

        def filter_rows(i, _):
            rows = pl.ds(pl.multiple_of(i * step_rows, step_rows), step_rows)
            total = None
            for tap in range(TAPS):
                at = s + tap - (TAPS - 1)
                weights = window[tap : tap + 1, :]
                if at < 0:
                    term = hist[TAPS - 1 + at, rows, :].astype(jnp.float32) * (weights * live)
                else:
                    term = frames[at, rows, :].astype(jnp.float32) * weights
                total = term if total is None else total + term
            filtered[rows, :] = total.astype(jnp.bfloat16)
            return 0

        lax.fori_loop(0, feed_dev // step_rows, filter_rows, 0)

        def transform(i, _):
            other = lax.rem(feed + 1 + i, feed_size)
            block = lax.dot_general(
                twiddle[other],
                filtered[...],
                (((1,), (1,)), ((), ())),
                preferred_element_type=jnp.float32,
            ).astype(jnp.bfloat16)

            @pl.when(other != feed)
            def _():
                send[s, other] = block
                spec_copy(s, other, feed).start()

            @pl.when(other == feed)
            def _():
                spec[s, other] = block

            return 0

        lax.fori_loop(0, feed_size, transform, 0)

    def make_tables():
        def one_hot(i, _):
            rows = pl.ds(pl.multiple_of(i * step_rows, step_rows), step_rows)
            shape = (step_rows, placed_v.shape[2])
            feeds = lax.broadcasted_iota(jnp.int32, shape, 0) + i * step_rows
            for m in range(placed_v.shape[0]):
                hit = feeds == slots[m : m + 1, :]
                placed_v[m, rows, :] = jnp.where(hit, 1.0, 0.0).astype(jnp.bfloat16)
            return 0

        lax.fori_loop(0, placed_v.shape[1] // step_rows, one_hot, 0)
        first = feed * chan_dev + CHANS
        chans = lax.broadcasted_iota(jnp.int32, (chan_dev, 4 * ews), 0) + first
        turns = sincos((ew_row[...] * chans) & (phase_modulus - 1), phase_modulus)
        for part, value in enumerate(turns):
            value = (value * 0.5).astype(jnp.bfloat16).astype(jnp.float32)
            steer[:, part * 4 * ews : (part + 1) * 4 * ews] = value
        centres, reach = coarse.shape[2], fine.shape[2]
        centre_ids = lax.broadcasted_iota(jnp.int32, (centres, ns_beams), 0) * (4 * reach)
        centre_ids = centre_ids + (2 * reach - 1)
        reach_ids = lax.broadcasted_iota(jnp.int32, (reach, ns_beams), 0) * 2 + 1
        half_modulus = 2 * phase_modulus
        factor = 1.0 / math.sqrt(ROWS)

        def rotations(c, _):
            step = (ns_row[...] * (first + c)) & (phase_modulus - 1)
            for ids, table, size in ((centre_ids, coarse, factor), (reach_ids, fine, 1.0)):
                re, im = sincos((ids * step) & (half_modulus - 1), half_modulus)
                table[0, c] = re * size
                table[1, c] = im * size
            return 0

        lax.fori_loop(0, chan_dev, rotations, 0)

    def arrive(s):
        def body(step, _):
            other = lax.rem(feed + step, feed_size)
            spec_copy(s, other, other).wait()
            return 0

        lax.fori_loop(1, feed_size, body, 0)

    def place(s):
        def body(m, _):
            total = jnp.zeros(grid.shape[1:], jnp.float32)
            for j in range(feed_size):
                total += jnp.dot(
                    spec[s, j],
                    placed_v[m, j * feed_dev : (j + 1) * feed_dev, :],
                    preferred_element_type=jnp.float32,
                )
            grid[m] = total
            return 0

        lax.fori_loop(0, grid.shape[0], body, 0)

    def mix_east(at):
        def body(i, _):
            start = pl.multiple_of(i * 8, 8)
            rows = pl.ds(start, 8)
            rows_im = pl.ds(pl.multiple_of(chan_dev + start, 8), 8)
            for pol in range(2):
                re = [grid[2 * y + pol, rows, :] for y in range(4)]
                im = [grid[2 * y + pol, rows_im, :] for y in range(4)]
                for e in range(ews):
                    sum_re = sum_im = None
                    for y in range(4):
                        w = e * 4 + y
                        w_re = steer[rows, w : w + 1]
                        w_im = steer[rows, 4 * ews + w : 4 * ews + w + 1]
                        term_re = w_re * re[y] - w_im * im[y]
                        term_im = w_re * im[y] + w_im * re[y]
                        sum_re = term_re if sum_re is None else sum_re + term_re
                        sum_im = term_im if sum_im is None else sum_im + term_im
                    row = at * 2 * pairs + pol * ews + e
                    east[rows, row, :] = sum_re
                    east[rows, row + pairs, :] = sum_im
            return 0

        lax.fori_loop(0, chan_dev // 8, body, 0)

    def mix_north(count):
        def channel(c):
            fine_re, fine_im = fine[0, c], fine[1, c]
            parts_re, parts_im = [], []
            for r in range(coarse.shape[2]):
                a_re, a_im = coarse[0, c, r : r + 1, :], coarse[1, c, r : r + 1, :]
                rr, ii, ri, ir = a_re * fine_re, a_im * fine_im, a_re * fine_im, a_im * fine_re
                parts_re.append(jnp.concatenate([rr - ii, rr + ii], axis=0).astype(jnp.bfloat16))
                parts_im.append(jnp.concatenate([ir + ri, ir - ri], axis=0).astype(jnp.bfloat16))
            side = east[c, : count * 2 * pairs, :].astype(jnp.bfloat16)
            by_re = jnp.dot(
                side, jnp.concatenate(parts_re, axis=0), preferred_element_type=jnp.float32
            )
            by_im = jnp.dot(
                side, jnp.concatenate(parts_im, axis=0), preferred_element_type=jnp.float32
            )
            for k in range(count):
                lo, mid, hi = 2 * k * pairs, (2 * k + 1) * pairs, (2 * k + 2) * pairs
                beam_re = by_re[lo:mid] - by_im[mid:hi]
                beam_im = by_re[mid:hi] + by_im[lo:mid]
                power[k, c] = beam_re * beam_re + beam_im * beam_im

        def body(i, _):
            for c in range(8):
                channel(i * 8 + c)
            return 0

        lax.fori_loop(0, chan_dev // 8, body, 0)

    def transpose_power(s, k):
        width = beam_dev * tm_size
        for e in range(ews):
            total = power[k, :, e, :] + power[k, :, ews + e, :]
            turned = total.T.astype(jnp.bfloat16)
            for part in range(ns_beams // beam_dev):
                first = e * ns_beams + part * beam_dev
                block = turned[part * beam_dev : (part + 1) * beam_dev]
                beams[first % width // beam_dev, first // width, s] = block

    def beam_copy(first, last, group, peer, slot):
        return pltpu.make_async_remote_copy(
            src_ref=beams.at[peer[0], peer[1], pl.ds(first, last - first)],
            dst_ref=out.at[slot[0], slot[1], pl.ds(first, last - first)],
            send_sem=beam_ss.at[group, peer[0], peer[1]],
            recv_sem=beam_rs.at[group, slot[0], slot[1]],
            device_id=peer,
            device_id_type=MESH,
        )

    middle = spec_dev // 2
    groups = [(spec_dev - 1, middle), (middle - 1, 0)]

    def form(group):
        high, low = groups[group]
        mix_north(high + 1 - low)
        for k, s in enumerate(range(low, high + 1)):
            transpose_power(s, k)

        def go(step, _):
            beam_copy(low, high + 1, group, other_device(step), (tm, feed)).start()
            return 0

        lax.fori_loop(1, tm_size * feed_size, go, 0)
        out[tm, feed, low : high + 1] = beams[tm, feed, low : high + 1]

    def gather_east(s):
        arrive(s)
        place(s)
        mix_east(s - middle if s >= middle else s)

    channelize(spec_dev - 1)
    make_tables()
    waiting = TAPS - 3
    for s in range(spec_dev - 2, -1, -1):
        if waiting >= 0:
            history(waiting + 1).wait_send()
            history(waiting).start()
            waiting -= 1
        channelize(s)
        if s + 1 > middle:
            gather_east(s + 1)
        if s == middle - 1:
            gather_east(middle)
    form(0)
    for s in range(middle - 1, -1, -1):
        gather_east(s)
    form(1)
    for group, (high, low) in enumerate(groups):
        def finish(step, _):
            peer = other_device(step)
            beam_copy(low, high + 1, group, peer, peer).wait()
            return 0

        lax.fori_loop(1, tm_size * feed_size, finish, 0)
    history(0).wait_send()


def search(voltages, slots, ew_row, ns_row, tm_size, feed_size, beam_dev):
    feed_dev = voltages.shape[0]
    spec_dev = voltages.shape[1] // NFFT
    chan_dev = CHANS // feed_size
    ns_beams = ns_row.shape[1]
    pairs = 2 * ew_row.shape[1] // 4
    window = jnp.asarray(window_constant(TAPS, NFFT))
    twiddle = jnp.asarray(dft_constant(NFFT, CHANS, feed_size))
    blocks = (spec_dev, feed_size, 2 * chan_dev, feed_dev)
    batch = spec_dev - spec_dev // 2
    vmem = pl.BlockSpec(memory_space=pltpu.VMEM)
    hbm = pl.BlockSpec(memory_space=pl.ANY)
    dma = pltpu.SemaphoreType.DMA
    sent = (tm_size, feed_size, spec_dev, beam_dev, chan_dev)
    return pl.pallas_call(
        search_kernel,
        out_shape=jax.ShapeDtypeStruct(sent, jnp.bfloat16),
        in_specs=[hbm, vmem, hbm, vmem, vmem, vmem],
        out_specs=vmem,
        scratch_shapes=[
            pltpu.VMEM((2, feed_dev, NFFT), jnp.int32),
            pltpu.VMEM((spec_dev, feed_dev, NFFT), jnp.bfloat16),
            pltpu.VMEM((TAPS - 1, feed_dev, NFFT), jnp.bfloat16),
            pltpu.VMEM((feed_dev, NFFT), jnp.bfloat16),
            pltpu.VMEM(blocks, jnp.bfloat16),
            pltpu.VMEM(blocks, jnp.bfloat16),
            pltpu.VMEM(twiddle.shape, jnp.bfloat16),
            pltpu.VMEM((slots.shape[0], slots.size, ROWS), jnp.bfloat16),
            pltpu.VMEM((slots.shape[0], 2 * chan_dev, ROWS), jnp.float32),
            pltpu.VMEM((chan_dev, batch * 2 * pairs, ROWS), jnp.float32),
            pltpu.VMEM((chan_dev, 2 * ew_row.shape[1]), jnp.float32),
            pltpu.VMEM((2, chan_dev, ROWS // (2 * REACH), ns_beams), jnp.float32),
            pltpu.VMEM((2, chan_dev, REACH, ns_beams), jnp.float32),
            pltpu.VMEM((batch, chan_dev, pairs, ns_beams), jnp.float32),
            pltpu.VMEM(sent, jnp.bfloat16),
            dma((2,)),
            dma(()),
            dma((TAPS - 1,)),
            dma((TAPS - 1,)),
            dma((spec_dev, feed_size)),
            dma((spec_dev, feed_size)),
            dma((2, tm_size, feed_size)),
            dma((2, tm_size, feed_size)),
        ],
        compiler_params=pltpu.CompilerParams(
            collective_id=0, has_side_effects=True, vmem_limit_bytes=60 * 1024 * 1024
        ),
        name="search",
    )(voltages, window, twiddle, slots, ew_row, ns_row)


def transform_table(spec_total):
    ids = np.outer(np.arange(1, spec_total // 2 + 1), np.arange(spec_total)) % spec_total
    turn = ids * (TWO_PI / spec_total)
    table = np.stack([np.cos(turn), -np.sin(turn)]) / math.sqrt(spec_total)
    return table.astype(jnp.bfloat16).astype(np.float64)


def dedisperse_kernel(series, delays, out, freq, phase, send, recv, result, send_s, recv_s):
    tm_size, feed_size, spec_dev, beam_dev, chan_dev = series.shape
    spec_total = spec_dev * tm_size
    half = spec_total // 2
    trials = delays.shape[1]
    trial_dev = trials // tm_size
    table = transform_table(spec_total)
    tm = lax.axis_index("tm")
    feed = lax.axis_index("feed")

    barrier = pltpu.get_barrier_semaphore()
    for step in range(1, tm_size):
        other = lax.rem(tm + step, tm_size)
        pl.semaphore_signal(barrier, inc=1, device_id=(other, feed), device_id_type=MESH)

    def to_frequency(f, _):
        lanes = pl.ds(pl.multiple_of(f * chan_dev, chan_dev), chan_dev)
        x = [
            series[t // spec_dev, f, t % spec_dev].astype(jnp.float32) for t in range(spec_total)
        ]
        even = [x[t] + x[spec_total - t] for t in range(1, half)]
        odd = [x[t] - x[spec_total - t] for t in range(1, half)]
        for k in range(half):
            re = x[0] * float(table[0, k, 0]) + x[half] * float(table[0, k, half])
            im = None
            for t in range(1, half):
                re = re + even[t - 1] * float(table[0, k, t])
                term = odd[t - 1] * float(table[1, k, t])
                im = term if im is None else im + term
            freq[k, :beam_dev, lanes] = re.astype(jnp.bfloat16)
            freq[k, beam_dev:, lanes] = im.astype(jnp.bfloat16)
        return 0

    lax.fori_loop(0, feed_size, to_frequency, 0)

    step_rows = 16

    def make_phase(i, _):
        rows = pl.ds(pl.multiple_of(i * step_rows, step_rows), step_rows)
        base_re, base_im = sincos(delays[rows, :] & (spec_total - 1), spec_total)
        re, im = base_re, base_im
        for k in range(half):
            phase[k, rows, :trials] = re.astype(jnp.bfloat16)
            phase[k, rows, trials:] = im.astype(jnp.bfloat16)
            re, im = re * base_re - im * base_im, re * base_im + im * base_re
        return 0

    lax.fori_loop(0, delays.shape[0] // step_rows, make_phase, 0)

    def move(k, _):
        mixed = jnp.dot(freq[k], phase[k], preferred_element_type=jnp.float32)
        factor = 1.0 / math.sqrt(CHANS)
        re = (mixed[:beam_dev, :trials] - mixed[beam_dev:, trials:]) * factor
        im = (mixed[:beam_dev, trials:] + mixed[beam_dev:, :trials]) * factor
        for u in range(tm_size):
            part = slice(u * trial_dev, (u + 1) * trial_dev)
            send[u, 2 * k] = re[:, part].astype(jnp.bfloat16)
            send[u, 2 * k + 1] = im[:, part].astype(jnp.bfloat16)
        return 0

    def exchange(part, other, slot):
        ids = pl.ds(part * half, half)
        return pltpu.make_async_remote_copy(
            src_ref=send.at[other, ids],
            dst_ref=recv.at[slot, ids],
            send_sem=send_s.at[part, other],
            recv_sem=recv_s.at[part, slot],
            device_id=(other, feed),
            device_id_type=MESH,
        )

    edges = (0, half // 2, half)
    pl.semaphore_wait(barrier, tm_size - 1)
    for part in range(2):
        lax.fori_loop(edges[part], edges[part + 1], move, 0)
        for step in range(1, tm_size):
            exchange(part, lax.rem(tm + step, tm_size), tm).start()
    recv[tm] = send[tm]
    for part in range(2):
        for step in range(1, tm_size):
            other = lax.rem(tm + step, tm_size)
            exchange(part, other, other).wait()

    def to_time(u, _):
        rows = pl.ds(pl.multiple_of(u * beam_dev, beam_dev), beam_dev)
        re = [recv[u, 2 * k].astype(jnp.float32) for k in range(half)]
        im = [recv[u, 2 * k + 1].astype(jnp.float32) for k in range(half)]
        for t in range(half + 1):
            by_re = by_im = None
            for k in range(half):
                weight = 1.0 if 2 * (k + 1) == spec_total else 2.0
                term_re = re[k] * float(table[0, k, t] * weight)
                term_im = im[k] * float(table[1, k, t] * weight)
                by_re = term_re if by_re is None else by_re + term_re
                by_im = term_im if by_im is None else by_im + term_im
            result[t, rows, :] = by_re + by_im
            if 0 < t < half:
                result[spec_total - t, rows, :] = by_re - by_im
        return 0

    lax.fori_loop(0, tm_size, to_time, 0)

    def turn(t, _):
        out[t] = result[t].T
        return 0

    lax.fori_loop(0, spec_total, turn, 0)


def dedisperse(series, delays):
    tm_size, feed_size, spec_dev, beam_dev, chan_dev = series.shape
    spec_total = spec_dev * tm_size
    half = spec_total // 2
    chans, trials = delays.shape
    trial_dev = trials // tm_size
    beams = beam_dev * tm_size
    blocks = (tm_size, 2 * half, beam_dev, trial_dev)
    vmem = pl.BlockSpec(memory_space=pltpu.VMEM)
    return pl.pallas_call(
        dedisperse_kernel,
        out_shape=jax.ShapeDtypeStruct((spec_total, trial_dev, beams), jnp.float32),
        in_specs=[vmem] * 2,
        out_specs=vmem,
        scratch_shapes=[
            pltpu.VMEM((half, 2 * beam_dev, chans), jnp.bfloat16),
            pltpu.VMEM((half, chans, 2 * trials), jnp.bfloat16),
            pltpu.VMEM(blocks, jnp.bfloat16),
            pltpu.VMEM(blocks, jnp.bfloat16),
            pltpu.VMEM((spec_total, beams, trial_dev), jnp.float32),
            pltpu.SemaphoreType.DMA((2, tm_size)),
            pltpu.SemaphoreType.DMA((2, tm_size)),
        ],
        compiler_params=pltpu.CompilerParams(
            collective_id=1, has_side_effects=True, vmem_limit_bytes=48 * 1024 * 1024
        ),
        name="dedisperse",
    )(series, delays)


def local(voltages, feed_at_grid_slot, ew_grid, ns_grid, delays):
    tm_size = lax.axis_size("tm")
    feed_size = lax.axis_size("feed")
    slots = feed_at_grid_slot.reshape(-1, 2, REACH, 8)
    slots = jnp.stack([slots[:, 1], slots[:, 0, ::-1]], axis=1).reshape(ROWS, 8).T
    ew_row = (ew_grid[:, None] * jnp.arange(4, dtype=jnp.int32)[None, :]).reshape(1, -1)
    ns_row = ns_grid.reshape(1, -1)
    beam_dev = ew_grid.shape[0] * ns_grid.shape[0] // (tm_size * feed_size)
    series = search(voltages, slots, ew_row, ns_row, tm_size, feed_size, beam_dev)
    return dedisperse(series, delays).transpose(1, 2, 0)


def solution(mesh):
    in_specs = (P("feed", "tm"), P(), P(), P(), P())
    out_specs = P("tm", "feed", None)
    aligned = CHANS // mesh.shape["feed"] % 128 == 0
    body = local if aligned else local_unaligned
    return jax.shard_map(body, mesh=mesh, in_specs=in_specs, out_specs=out_specs, check_vma=False)
```
